128 devices in a mesh: dp: 4 (over x), ctx: 8 (over z, core), exp: 4 (over y).
Axes of the slice: x: 4, y: 4, z: 4, core: 2. Of those that a mesh axis runs over, the one named last changes fastest.
Arguments:
- states: bfloat16 [65536, 2048], P(('dp', 'ctx'), 'exp'), parts along dimension 0
- chosen: int32 [16384], P('dp'), parts along dimension 0, may hold values from 0 to 2047, as said below
- counts: int32 [32], P('dp'), parts along dimension 0, may hold values from 64 to 512, as said below
- attn_gain: float32 [2048], replicated, may hold values from 0.1 to 1.9
- query_weight: bfloat16 [2048, 2048], P(None, 'exp'), as said below
- key_weight: bfloat16 [2048, 2048], P(None, 'exp'), as said below
- value_weight: bfloat16 [2048, 2048], P(None, 'exp'), may hold values from -0.5 to 0.5
- out_weight: bfloat16 [2048, 2048], P('exp'), may hold values from -0.125 to 0.125
- moe_gain: float32 [2048], replicated, may hold values from 0.1 to 1.9
- routes: int32 [16384, 8], P(('dp', 'ctx', 'exp')), parts along dimension 0, may hold values from 0 to 31, all different within a row; in each aligned block of 128 rows (0 to 127, 128 to 255, ...) at most 48 rows name the same one
- gate_probs: float32 [16384, 8], P(('dp', 'ctx', 'exp')), parts along dimension 0, may hold values from 0.05 to 0.5
- w_gate: bfloat16 [32, 2048, 1024], P(('ctx', 'exp')), may hold values from -0.125 to 0.125
- w_up: bfloat16 [32, 2048, 1024], P(('ctx', 'exp')), may hold values from -0.125 to 0.125
- w_down: bfloat16 [32, 1024, 2048], P(('ctx', 'exp')), may hold values from -0.1875 to 0.1875
Outputs:
- block_out: bfloat16 [65536, 2048], P(('dp', 'ctx'), 'exp'), parts along dimension 0
The draws below stay inside these ranges and needn't reach their ends.
There are 4 independent parts, one for each index of `dp`. The reference program is written for one: setup_inputs(seed, part) draws one part's arguments, and reference() takes and returns one part's arrays. A program takes and returns all parts, laid end to end along the dimension named above; an argument that names none is the same for every part. Nothing has to cross between parts.
Inputs may be any that keep to these rules, and one draw needn't show every extreme that they name: `chosen`: in shard s the first counts[s] slots (from s * 512) hold distinct positions of that shard in rising order; the others hold 0. `counts`: some shard has 512 live slots. `routes`: in each aligned block of 128 rows no expert is named by more than 48 rows. `query_weight`: projection weights. `key_weight`: projection weights.
All inputs are finite; a program needn't handle non-finite values.
Results may differ from the reference program's by a relative error of at most 0.017.
Values may be sent and summed in bfloat16 or wider, within the bound.
No kernel may reach another device: no remote copies, remote signals or barrier semaphores. Data moves between devices by JAX's collectives and lax.ppermute only.
A program may use at most 128 MiB of HBM per device.

```python
import math
import jax
import jax.numpy as jnp
import numpy as np
from jax import lax

D = 2048
HEADS = 16
HEAD_DIM = 128
FF = 1024
TOP = 8
POS_DEV = 2048
CAP = 512
R = 128
EXPERTS = 32
MOST = 48
SLOTS = 4096
LENGTH = 16384


def shard_lists(key):
    key = jax.random.fold_in(key, 11)
    shards = SLOTS // CAP
    count_key, full_key, place_key = jax.random.split(key, 3)
    drawn = jax.random.randint(count_key, (shards,), CAP // 8, 7 * CAP // 8 + 1)
    full_shard = jax.random.randint(full_key, (), 0, shards)
    counts = jnp.where(jnp.arange(shards) == full_shard, CAP, drawn).astype(jnp.int32)

    def one_shard(subkey, count):
        order = jax.random.permutation(subkey, POS_DEV)[:CAP].astype(jnp.int32)
        slot_ids = jnp.arange(CAP, dtype=jnp.int32)
        keyed = jnp.where(slot_ids < count, order, POS_DEV)
        ordered = jnp.sort(keyed)
        return jnp.where(slot_ids < count, ordered, 0).astype(jnp.int32)
    chosen = jax.vmap(one_shard)(jax.random.split(place_key, shards), counts)
    return (counts, chosen.reshape(-1))


def base_projection(key):
    return jax.random.normal(jax.random.fold_in(key, 17), (D, HEADS * HEAD_DIM), jnp.float32)


def draw_chosen(key, part):
    lists = shard_lists(key)
    return lists[1]


def draw_counts(key, part):
    lists = shard_lists(key)
    return lists[0]


def draw_states(key, part):
    key = jax.random.fold_in(key, 5)
    return jax.random.normal(key, (LENGTH, D), jnp.float32).astype(jnp.bfloat16)


def draw_query_weight(key, part):
    base = base_projection(key)
    return (base * D ** (-0.5)).astype(jnp.bfloat16)


def draw_key_weight(key, part):
    key = jax.random.fold_in(key, 9)
    fresh = jax.random.normal(key, (D, HEADS * HEAD_DIM), jnp.float32)
    return (fresh * D ** (-0.5)).astype(jnp.bfloat16)


def block_scale(key, extent, pieces, low, top_value):
    def one(position, blocks):
        draws = jax.random.uniform(jax.random.fold_in(jax.random.fold_in(key, 6), position), (blocks,), jnp.float32, low / len(pieces), top_value / len(pieces))
        return jnp.repeat(jnp.exp(draws), extent[position] // blocks).reshape((-1,) + (1,) * (len(extent) - position - 1))

    loudness = one(*pieces[0])
    for cut in pieces[1:]:
        loudness = loudness * one(*cut)
    return loudness


def assign_block(key, own, number, rows, amount, top, most, skew):
    sequence = jax.random.permutation(key, amount)
    crowded, ordinary = portions_of(amount, rows * top, most, skew, True), portions_of(amount, rows * top, most, skew, False)
    places = jnp.arange(amount)

    def named(tallies, offset_by):
        used = int((tallies > 0).sum())
        fixed = max(1, used // 4)
        passed = fixed + (places - fixed + offset_by * (used - fixed)) % max(1, amount - fixed)
        return jnp.zeros((amount,), jnp.int32).at[sequence[jnp.where(places < fixed, places, passed)]].set(jnp.asarray(tallies, jnp.int32))

    tallies = jnp.where(number % 4 == 0, named(crowded, number // 4), named(ordinary, number - number // 4 - 1))
    mixed = jax.random.permutation(jax.random.fold_in(own, 3), amount)
    giver, sink = mixed[0:amount // 2 * 2:2], mixed[1:amount // 2 * 2:2]
    margin = jnp.minimum(tallies[giver] - 1, most - tallies[sink]) // 2
    margin = jnp.where((giver == sequence[0]) | (sink == sequence[0]) | (tallies[sink] == 0), 0, jnp.maximum(margin, 0))
    passed = jax.random.randint(jax.random.fold_in(own, 4), (amount // 2,), 0, 1 << 20) % (margin + 1)
    tallies = tallies.at[giver].add(-passed).at[sink].add(passed)
    labels = jnp.searchsorted(jnp.cumsum(tallies), jnp.arange(rows * top), side="right").astype(jnp.int32)
    listing = labels.reshape(top, rows).T
    listing = listing[jax.random.permutation(jax.random.fold_in(own, 1), rows)]
    offset_by = jax.random.randint(jax.random.fold_in(own, 2), (rows, 1), 0, top)
    return jnp.take_along_axis(listing, (jnp.arange(top)[None, :] + offset_by) % top, axis=1)


def portions_of(amount, total, most, slope, full):
    weights = [(1 << 20) // math.isqrt(grade ** slope) + 1 for grade in range(1, amount + 1)]
    largest = most if full else min(most, max(-(-total // amount), total * weights[0] // sum(weights)))
    least = 1 if total - largest >= amount - 1 else 0
    given, spare = [largest] + [least] * (amount - 1), total - largest - least * (amount - 1)
    while spare > 0:
        movable = [i for i in range(1, amount) if given[i] < largest] or [i for i in range(1, amount) if given[i] < most]
        whole, remaining = sum([weights[i] for i in movable]), spare
        for i in movable:
            more = min(most - given[i], max(1, remaining * weights[i] // whole), spare)
            given[i] = given[i] + more
            spare = spare - more
    return np.array(given)


def scatter_about(own_key, dims, deviation, most, cuts=(), held_as=jnp.bfloat16):
    loudness = block_scale(own_key, dims, cuts, -0.22, 0.18) if cuts else 1.0
    array = jax.random.normal(own_key, dims, jnp.float32) * deviation * loudness
    return jnp.minimum(jnp.maximum(array, -most), most).astype(held_as)


def setup_inputs(seed: int = 0, part: int = 0) -> dict:
    streams_of = jax.random.split(jax.random.key(seed), 15)
    own_keys = jax.random.split(jax.random.fold_in(streams_of[14], part), 15)
    states = draw_states(jax.random.fold_in(jax.random.fold_in(streams_of[14], part), 71), part)
    chosen = draw_chosen(jax.random.fold_in(jax.random.fold_in(streams_of[14], part), 71), part)
    counts = draw_counts(jax.random.fold_in(jax.random.fold_in(streams_of[14], part), 71), part)
    attn_gain = jnp.clip(1.0 + 0.18 * jax.random.normal(streams_of[3], (D,), jnp.float32), 0.1, 1.9)
    query_weight = draw_query_weight(jax.random.fold_in(streams_of[14], 71), part)
    key_weight = draw_key_weight(jax.random.fold_in(streams_of[14], 71), part)
    value_weight = scatter_about(streams_of[6], (D, HEADS * HEAD_DIM), (D // 16) ** -0.5, 0.5, ((1, 4),))
    out_weight = scatter_about(streams_of[7], (HEADS * HEAD_DIM, D), (HEADS * HEAD_DIM) ** -0.5, 0.125, ((0, 4),))
    moe_gain = jnp.clip(1.0 + 0.18 * jax.random.normal(streams_of[8], (D,), jnp.float32), 0.1, 1.9)
    routes_keys = jax.random.split(jax.random.fold_in(own_keys[9], 1), SLOTS // R)
    routes_turns = jax.random.permutation(jax.random.fold_in(own_keys[9], 3), SLOTS // R)
    routes = jax.vmap(lambda own, number: assign_block(jax.random.fold_in(own_keys[9], 2), own, number, R, EXPERTS, TOP, MOST, 2))(routes_keys, routes_turns).reshape((SLOTS, TOP))
    gate_probs = jnp.clip(jnp.exp(math.log(0.5) - 2.3025851 * jax.random.uniform(own_keys[10], (SLOTS, TOP), jnp.float32) ** block_scale(own_keys[10], (SLOTS, TOP), ((0, 32),), -0.2, 0.2)), 0.05, 0.5)
    w_gate = scatter_about(streams_of[11], (EXPERTS, D, FF), D ** -0.5, 0.125, ((0, 32),))
    w_up = scatter_about(streams_of[12], (EXPERTS, D, FF), D ** -0.5, 0.125, ((0, 32),))
    w_down = scatter_about(streams_of[13], (EXPERTS, FF, D), FF ** -0.5, 0.1875, ((0, 32),))
    return dict(states=states, chosen=chosen, counts=counts, attn_gain=attn_gain, query_weight=query_weight, key_weight=key_weight, value_weight=value_weight, out_weight=out_weight, moe_gain=moe_gain, routes=routes, gate_probs=gate_probs, w_gate=w_gate, w_up=w_up, w_down=w_down)


def rms_rows(values, gain):
    wide = values.astype(jnp.float32)
    factor = lax.rsqrt(lax.optimization_barrier(jnp.mean(wide * wide, axis=-1, keepdims=True)) + 1e-05)
    return (wide * factor * gain).astype(jnp.bfloat16)

def reference(states, chosen, counts, attn_gain, query_weight, key_weight, value_weight, out_weight, moe_gain, routes, gate_probs, w_gate, w_up, w_down):
    index = jnp.arange(SLOTS, dtype=jnp.int32)
    shard = index // CAP
    limit = counts[shard]
    live = index % CAP < limit
    place = (shard * POS_DEV + chosen).astype(jnp.int32)
    rows = states[place]
    normed = rms_rows(rows, attn_gain)
    queries = jnp.dot(normed, query_weight, preferred_element_type=jnp.float32).astype(jnp.bfloat16)
    key_rows = jnp.dot(normed, key_weight, preferred_element_type=jnp.float32).astype(jnp.bfloat16)
    value_rows = jnp.dot(normed, value_weight, preferred_element_type=jnp.float32).astype(jnp.bfloat16)
    score_scale = 1.0 / HEAD_DIM ** 0.5
    allowed = live[None, :] & (place[None, :] <= place[:, None])

    def one_head(head):
        start = (head * HEAD_DIM).astype(jnp.int32)
        query_head = lax.dynamic_slice_in_dim(queries, start, HEAD_DIM, 1)
        key_head = lax.dynamic_slice_in_dim(key_rows, start, HEAD_DIM, 1)
        value_head = lax.dynamic_slice_in_dim(value_rows, start, HEAD_DIM, 1)
        scores = jnp.dot(query_head, key_head.T, preferred_element_type=jnp.float32) * score_scale
        row_peak = lax.optimization_barrier(jnp.max(jnp.where(allowed, scores, -1e+30), axis=1, keepdims=True))
        weights = jnp.where(allowed, jnp.exp(scores - row_peak), 0.0)
        row_mass = jnp.where(live, lax.optimization_barrier(jnp.sum(weights, axis=1)), 1.0)
        summed = jnp.dot(weights.astype(jnp.bfloat16), value_head, preferred_element_type=jnp.float32)
        return summed / row_mass[:, None]
    heads_out = lax.map(one_head, jnp.arange(HEADS, dtype=jnp.int32))
    attended = jnp.transpose(heads_out, (1, 0, 2)).reshape(SLOTS, HEADS * HEAD_DIM).astype(jnp.bfloat16)
    hidden = (rows.astype(jnp.float32) + jnp.dot(attended, out_weight, preferred_element_type=jnp.float32)).astype(jnp.bfloat16)
    normed2 = rms_rows(hidden, moe_gain)
    bound = MOST * (SLOTS // R)

    def one_expert(total, expert):
        named = routes == expert
        taken = jnp.any(named, axis=1) & live
        weight = lax.optimization_barrier(jnp.sum(jnp.where(named, gate_probs, 0.0), axis=1))
        order = jnp.argsort(jnp.where(taken, 0, 1).astype(jnp.int32), stable=True)[:bound].astype(jnp.int32)
        valid = taken[order]
        picked = normed2[order]
        gate_part = jnp.dot(picked, w_gate[expert], preferred_element_type=jnp.float32)
        up_part = jnp.dot(picked, w_up[expert], preferred_element_type=jnp.float32)
        act = (jax.nn.silu(gate_part) * up_part).astype(jnp.bfloat16)
        expert_out = jnp.dot(act, w_down[expert], preferred_element_type=jnp.float32).astype(jnp.bfloat16)
        scaled = jnp.where(valid, weight[order], 0.0)[:, None] * expert_out.astype(jnp.float32)
        return (total.at[order].add(scaled), None)
    total, _ = lax.scan(one_expert, jnp.zeros((SLOTS, D), jnp.float32), jnp.arange(EXPERTS, dtype=jnp.int32))
    merged = (hidden.astype(jnp.float32) + total).astype(jnp.bfloat16)
    target = jnp.where(live, place, LENGTH).astype(jnp.int32)
    return states.at[target].set(merged, mode='drop')
```

```python
import jax
import jax.numpy as jnp
from jax import lax
from jax.experimental import pallas as pl
from jax.experimental.pallas import tpu as pltpu
from jax.sharding import Mesh, PartitionSpec as P

HEAD = 128
ROW = 128
MOST = 48
TILE = 256
REGION = 1088
EPS = 1e-05
RING = 4
F32 = jnp.float32
BF16 = jnp.bfloat16
OFFSETS = (
    (0, 0),
    (-1, 0),
    (1, 0),
    (0, -1),
    (0, 1),
    (2, 0),
    (0, 2),
    (-1, -1),
    (-1, 1),
    (1, -1),
    (1, 1),
    (-1, 2),
    (1, 2),
    (2, -1),
    (2, 1),
    (2, 2),
)
PIECES = tuple(((block, 0, ROW),) for block in range(7)) + (
    ((7, 0, 64), (8, 0, 64)),
    ((9, 0, 64), (10, 0, 64)),
    ((7, 64, 64), (9, 64, 64)),
    ((8, 64, 64), (10, 64, 64)),
    ((11, 0, ROW),),
    ((12, 0, ROW),),
    ((13, 0, ROW),),
    ((14, 0, ROW),),
    ((15, 0, 64),),
    ((15, 64, 64),),
)
HBM = pl.BlockSpec(memory_space=pl.ANY)
VMEM = pl.BlockSpec(memory_space=pltpu.VMEM)
SMEM = pl.BlockSpec(memory_space=pltpu.SMEM)


def dot(left, right):
    return jnp.dot(left, right, preferred_element_type=F32)


def shift(value, axis, step):
    return lax.ppermute(value, axis, [(i, (i + step) % RING) for i in range(RING)])


def ring_all(value, axis):
    return [value] + [shift(value, axis, step) for step in range(1, RING)]


def swap(value):
    return lax.ppermute(value, "core", [(0, 1), (1, 0)])


def rms(wide, gain):
    factor = lax.rsqrt(jnp.mean(wide * wide, axis=-1, keepdims=True) + EPS)
    return (wide * factor * gain).astype(BF16)


def project_kernel(info, own, left, right, far_top, far_bottom, gain, wq, wk, wv, *rest):
    outs, base, rows, normed, weights, made, sems = (
        rest[:4],
        rest[4],
        rest[5],
        rest[6],
        rest[7],
        rest[8],
        rest[9],
    )
    z, y = info[0], info[1]
    slots = rows.shape[0]
    part = own.shape[1]
    half = slots // 2

    def columns(step):
        return pl.ds(pl.multiple_of(lax.rem(y + step, RING) * part, part), part)

    copies = [
        pltpu.make_async_copy(own, rows.at[:, columns(0)], sems.at[0]),
        pltpu.make_async_copy(left, rows.at[:, columns(3)], sems.at[1]),
        pltpu.make_async_copy(right, rows.at[:, columns(1)], sems.at[2]),
        pltpu.make_async_copy(far_top, rows.at[pl.ds(0, half), columns(2)], sems.at[3]),
        pltpu.make_async_copy(far_bottom, rows.at[pl.ds(half, half), columns(2)], sems.at[4]),
    ]
    loads = [
        pltpu.make_async_copy(w, weights.at[i], sems.at[5 + i]) for i, w in enumerate((wq, wk, wv))
    ]
    for copy in copies + loads:
        copy.start()
    for copy in copies:
        copy.wait()

    def norm(step, _):
        at = pl.ds(pl.multiple_of(step * 64, 64), 64)
        normed[at, :] = rms(rows[at, :].astype(F32), gain[...])
        return 0

    lax.fori_loop(0, slots // 64, norm, 0)
    base[...] = rows[pl.ds(pl.multiple_of(y * ROW, ROW), ROW), :]
    for i in range(3):
        loads[i].wait()

        def chunk(step, _, i=i):
            at = pl.ds(pl.multiple_of(step * 256, 256), 256)
            made[at, :] = dot(normed[at, :], weights[i]).astype(BF16)
            return 0

        lax.fori_loop(0, slots // 256, chunk, 0)
        for step, out in enumerate(outs):
            head = lax.rem(z + step, RING)
            out[:, i * HEAD : (i + 1) * HEAD] = made[
                :, pl.ds(pl.multiple_of(head * HEAD, HEAD), HEAD)
            ]


def project(info, pieces, gain, wq, wk, wv):
    slots, part = pieces[0].shape
    width = gain.shape[-1]
    return pl.pallas_call(
        project_kernel,
        out_shape=[jax.ShapeDtypeStruct((slots, 3 * HEAD), BF16)] * RING
        + [jax.ShapeDtypeStruct((ROW, width), BF16)],
        in_specs=[SMEM] + [HBM] * 5 + [VMEM] + [HBM] * 3,
        out_specs=[VMEM] * 5,
        scratch_shapes=[
            pltpu.VMEM((slots, width), BF16),
            pltpu.VMEM((slots, width), BF16),
            pltpu.VMEM((3, width, part), BF16),
            pltpu.VMEM((slots, part), BF16),
            pltpu.SemaphoreType.DMA((8,)),
        ],
        compiler_params=pltpu.CompilerParams(vmem_limit_bytes=32 * 2**20),
        cost_estimate=pl.CostEstimate(
            flops=6 * slots * width * part, bytes_accessed=12 * 2**20, transcendentals=0
        ),
        name="project",
    )(info, *pieces, gain, wq, wk, wv)


def attend_kernel(info, *rest):
    mine, theirs, out = rest[:4], rest[4:8], rest[8]
    held, sems = rest[9], rest[10]
    z, core = info[0], info[2]
    slots = held.shape[1]
    scale = 1.0 / HEAD**0.5
    copies = []
    for step in range(RING):
        chip = lax.rem(z + RING - step, RING)
        copies.append(
            pltpu.make_async_copy(mine[step], held.at[2 * chip + core], sems.at[2 * step])
        )
        copies.append(
            pltpu.make_async_copy(theirs[step], held.at[2 * chip + 1 - core], sems.at[2 * step + 1])
        )
    for copy in copies:
        copy.start()
    for copy in copies:
        copy.wait()

    def fold(carry, query, shard, mask):
        peak, mass, total = carry
        keys = held[shard, :, HEAD : 2 * HEAD]
        values = held[shard, :, 2 * HEAD :]
        scores = (
            lax.dot_general(query, keys, (((1,), (1,)), ((), ())), preferred_element_type=F32)
            * scale
        )
        scores = jnp.where(mask, scores, -1e30)
        peak_new = jnp.maximum(peak, jnp.max(scores, axis=1, keepdims=True))
        weights = jnp.exp(scores - peak_new)
        shrink = jnp.exp(peak - peak_new)
        mass = mass * shrink + jnp.sum(weights, axis=1, keepdims=True)
        total = total * shrink + dot(weights.astype(BF16), values)
        return peak_new, mass, total

    def tile(chip, start, rows):
        own = 2 * chip + core
        query = held[own, start : start + rows, 0:HEAD]
        slot = lax.broadcasted_iota(jnp.int32, (rows, slots), 1)
        place = lax.broadcasted_iota(jnp.int32, (rows, slots), 0) + start
        carry = (
            jnp.full((rows, 1), -1e30, F32),
            jnp.zeros((rows, 1), F32),
            jnp.zeros((rows, HEAD), F32),
        )
        carry = fold(carry, query, own, (slot <= place) & (slot < info[3 + own]))
        carry = lax.fori_loop(
            0, own, lambda s, state: fold(state, query, s, slot < info[3 + s]), carry
        )
        out[chip, start : start + rows, :] = (carry[2] / carry[1]).astype(BF16)

    def shard(chip, _):
        live = info[3 + 2 * chip + core]
        half = slots // 2

        @pl.when(live > half)
        def _():
            tile(chip, 0, slots)

        @pl.when(live <= half)
        def _():
            tile(chip, 0, half)
            out[chip, half:, :] = jnp.zeros((half, HEAD), BF16)

        return 0

    lax.fori_loop(0, RING, shard, 0)


def attend(info, mine, theirs):
    slots = mine[0].shape[0]
    return pl.pallas_call(
        attend_kernel,
        out_shape=jax.ShapeDtypeStruct((RING, slots, HEAD), BF16),
        in_specs=[SMEM] + [HBM] * 8,
        out_specs=VMEM,
        scratch_shapes=[
            pltpu.VMEM((2 * RING, slots, 3 * HEAD), BF16),
            pltpu.SemaphoreType.DMA((8,)),
        ],
        compiler_params=pltpu.CompilerParams(vmem_limit_bytes=32 * 2**20),
        cost_estimate=pl.CostEstimate(
            flops=20 * slots * slots * 4 * HEAD,
            bytes_accessed=4 * 2**20,
            transcendentals=20 * slots * slots,
        ),
        name="attend",
    )(info, *mine, *theirs)


def mix_kernel(pieces, base, gain, weight, hidden, normed, heads, total, held, sems):
    parts, _, width = weight.shape
    copies = [pltpu.make_async_copy(weight.at[i], held.at[i], sems.at[i]) for i in range(parts)]
    for copy in copies:
        copy.start()
    for z in range(RING):
        for y in range(RING):
            at = (y * RING + z) * HEAD
            heads[:, at : at + HEAD] = pieces[z * RING + y]
    for i, copy in enumerate(copies):
        copy.wait()
        at = slice(i * width, (i + 1) * width)
        total[:, at] = base[:, at].astype(F32) + dot(heads[...], held[i])
    made = total[...].astype(BF16)
    hidden[...] = made
    normed[...] = rms(made.astype(F32), gain[...])


def mix(pieces, weight, base, gain):
    parts, depth, width = weight.shape
    whole = parts * width
    return pl.pallas_call(
        mix_kernel,
        out_shape=[jax.ShapeDtypeStruct((ROW, whole), BF16)] * 2,
        in_specs=[VMEM, VMEM, VMEM, HBM],
        out_specs=[VMEM] * 2,
        scratch_shapes=[
            pltpu.VMEM((ROW, depth), BF16),
            pltpu.VMEM((ROW, whole), F32),
            pltpu.VMEM((parts, depth, width), BF16),
            pltpu.SemaphoreType.DMA((parts,)),
        ],
        compiler_params=pltpu.CompilerParams(vmem_limit_bytes=32 * 2**20),
        cost_estimate=pl.CostEstimate(
            flops=2 * ROW * depth * whole, bytes_accessed=10 * 2**20, transcendentals=0
        ),
        name="mix",
    )(pieces, base, gain, weight)


def expert_kernel(segments, pick, spread, worth, *rest):
    count = len(PIECES)
    tokens, rest = rest[:count], rest[count:]
    weights, rest = rest[:6], rest[6:]
    outs, rest = rest[:count], rest[count:]
    held, chosen, act, scale, gates, ups, downs, token_sems, weight_sems = rest
    blocks = held.shape[0]
    width = held.shape[2]
    ff = act.shape[1]

    def views(refs, back):
        found = [[] for _ in range(blocks)]
        sem = 0
        for ref, piece in zip(refs, PIECES):
            at = 0
            for block, first, rows in piece:
                here = held.at[block, pl.ds(first, rows), :]
                there = ref.at[pl.ds(at, rows), :]
                source, target = (here, there) if back else (there, here)
                found[block].append(pltpu.make_async_copy(source, target, token_sems.at[sem]))
                at += rows
                sem += 1
        return found

    arriving = views(tokens, False)
    for block in arriving:
        for copy in block:
            copy.start()
    loads = []
    for q in range(2):
        for i, place in enumerate((gates, ups, downs)):
            loads.append(
                pltpu.make_async_copy(
                    weights[3 * q + i].at[0], place.at[q], weight_sems.at[3 * q + i]
                )
            )
    for copy in loads:
        copy.start()

    for j in range(blocks):
        for copy in arriving[j]:
            copy.wait()
        starts = [pl.multiple_of(segments[q * blocks + j], 16) for q in range(2)]
        for q in range(2):
            scale[pl.ds(starts[q], MOST), :] = worth[j, q * MOST : (q + 1) * MOST, :]
        for cut in range(width // 512):
            columns = slice(cut * 512, (cut + 1) * 512)
            got = dot(pick[j], held[j, :, columns]).astype(BF16)
            for q in range(2):
                chosen[pl.ds(starts[q], MOST), columns] = got[q * MOST : (q + 1) * MOST]
    for q in range(2):
        end = pl.multiple_of(segments[2 * blocks + q], 16)
        chosen[pl.ds(end, TILE + MOST), :] = jnp.zeros((TILE + MOST, width), BF16)
        scale[pl.ds(end, TILE + MOST), :] = jnp.zeros((TILE + MOST, ROW), F32)

    for q in range(2):
        for copy in loads[3 * q : 3 * q + 3]:
            copy.wait()

        def tile(start, rows, q=q):
            at = pl.ds(pl.multiple_of(q * REGION + start, 64), rows)
            for f in range(ff // 256):
                columns = slice(f * 256, (f + 1) * 256)
                x = chosen[at, :]
                gate = dot(x, gates[q, :, columns])
                up = dot(x, ups[q, :, columns])
                act[:rows, columns] = (gate / (1.0 + jnp.exp(-gate)) * up).astype(BF16)
            for f in range(width // 512):
                columns = slice(f * 512, (f + 1) * 512)
                made = dot(act[:rows, :], downs[q, :, columns])
                chosen[at, columns] = (made * scale[at, 0:1]).astype(BF16)

        def whole(t, _):
            tile(t * TILE, TILE)
            return 0

        used = segments[2 * blocks + q] - q * REGION
        full = lax.div(used + TILE // 2 - 1, TILE)
        lax.fori_loop(0, full, whole, 0)

        @pl.when(used > full * TILE)
        def _():
            tile(full * TILE, TILE // 2)

    leaving = views(outs, True)
    for j in range(blocks):
        starts = [pl.multiple_of(segments[q * blocks + j], 16) for q in range(2)]
        for cut in range(width // 512):
            columns = slice(cut * 512, (cut + 1) * 512)
            made = jnp.concatenate([chosen[pl.ds(at, MOST), columns] for at in starts], axis=0)
            held[j, :, columns] = dot(spread[j], made).astype(BF16)
        for copy in leaving[j]:
            copy.start()
    for block in leaving:
        for copy in block:
            copy.wait()


def experts(segments, pick, spread, worth, pieces, weights):
    width = pieces[0].shape[1]
    ff = weights[0].shape[2]
    blocks = len(OFFSETS)
    cuts = sum(len(piece) for piece in PIECES)
    return pl.pallas_call(
        expert_kernel,
        out_shape=[jax.ShapeDtypeStruct(p.shape, BF16) for p in pieces],
        in_specs=[SMEM, VMEM, VMEM, VMEM] + [HBM] * (len(pieces) + 6),
        out_specs=[HBM] * len(pieces),
        scratch_shapes=[
            pltpu.VMEM((blocks, ROW, width), BF16),
            pltpu.VMEM((2 * REGION, width), BF16),
            pltpu.VMEM((TILE, ff), BF16),
            pltpu.VMEM((2 * REGION, ROW), F32),
            pltpu.VMEM((2, width, ff), BF16),
            pltpu.VMEM((2, width, ff), BF16),
            pltpu.VMEM((2, ff, width), BF16),
            pltpu.SemaphoreType.DMA((cuts,)),
            pltpu.SemaphoreType.DMA((6,)),
        ],
        compiler_params=pltpu.CompilerParams(vmem_limit_bytes=56 * 2**20),
        cost_estimate=pl.CostEstimate(
            flops=2 * 1024 * width * ff * 3, bytes_accessed=42 * 2**20, transcendentals=2**20
        ),
        name="experts",
    )(segments, pick, spread, worth, *pieces, *weights)


def collect(own):
    half = ROW // 2
    left, right = shift(own, "exp", 1), shift(own, "exp", -1)
    below, above = shift(own, "z", 1), shift(own, "z", -1)
    far_y, far_z = shift(own, "exp", 2), shift(own, "z", 2)
    tops = jnp.concatenate([below[:half], above[:half]], axis=0)
    bottoms = jnp.concatenate([left[half:], right[half:]], axis=0)
    return [
        own,
        left,
        right,
        below,
        above,
        far_y,
        far_z,
        shift(tops, "exp", 1),
        shift(tops, "exp", -1),
        shift(bottoms, "z", 1),
        shift(bottoms, "z", -1),
        shift(far_z, "exp", 1),
        shift(far_z, "exp", -1),
        shift(far_y, "z", 1),
        shift(far_y, "z", -1),
        shift(far_z[:half], "exp", 2),
        shift(far_y[half:], "z", 2),
    ]


def add(first, *others):
    total = first.astype(F32)
    for other in others:
        total = total + other.astype(F32)
    return total


def give_back(pieces):
    half = ROW // 2
    own, left, right, below, above, far_y, far_z = pieces[:7]
    from_right = shift(pieces[11], "exp", -1)
    from_left = shift(pieces[12], "exp", 1)
    from_above = shift(pieces[13], "z", -1)
    from_below = shift(pieces[14], "z", 1)
    corner_top = shift(pieces[15], "exp", 2)
    corner_bottom = shift(pieces[16], "z", 2)
    tops = [shift(pieces[7], "exp", -1), shift(pieces[8], "exp", 1)]
    bottoms = [shift(pieces[9], "z", -1), shift(pieces[10], "z", 1)]

    def joined(base, top, bottom):
        return jnp.concatenate([add(base[:half], *top), add(base[half:], *bottom)], axis=0).astype(
            BF16
        )

    far_z = joined(
        far_z,
        [from_right[:half], from_left[:half], corner_top],
        [from_right[half:], from_left[half:]],
    )
    far_y = joined(
        far_y,
        [from_above[:half], from_below[:half]],
        [from_above[half:], from_below[half:], corner_bottom],
    )
    below = joined(below, [t[:half] for t in tops], [])
    above = joined(above, [t[half:] for t in tops], [])
    left = joined(left, [], [b[:half] for b in bottoms])
    right = joined(right, [], [b[half:] for b in bottoms])
    return add(
        own,
        shift(left, "exp", -1),
        shift(right, "exp", 1),
        shift(below, "z", -1),
        shift(above, "z", 1),
        shift(far_y, "exp", 2),
        shift(far_z, "z", 2),
    )


def on_device(
    states,
    chosen,
    counts,
    attn_gain,
    query_weight,
    key_weight,
    value_weight,
    out_weight,
    moe_gain,
    routes,
    gate_probs,
    w_gate,
    w_up,
    w_down,
):
    x, z = lax.axis_index("dp"), lax.axis_index("z")
    core, y = lax.axis_index("core"), lax.axis_index("exp")
    pos_dev, part = states.shape
    slots = chosen.shape[0] // (2 * RING)
    width = attn_gain.shape[0]
    shard = 2 * z + core
    info = jnp.concatenate([jnp.stack([z, y, core]), counts]).astype(jnp.int32)

    weights = [w_gate, w_up, w_down]
    swapped = [swap(w) for w in weights]
    cut = width // 8
    out_part = lax.dynamic_slice_in_dim(out_weight, (2 * x + core) * cut, cut, 1)
    out_part = lax.all_gather(out_part, "exp", axis=0, tiled=True)
    table = jnp.concatenate([routes.astype(F32), gate_probs], axis=1)
    table = jnp.stack(ring_all(table, "exp"))

    own_slots = lax.dynamic_slice_in_dim(chosen, shard * slots, slots)
    live = jnp.arange(slots, dtype=jnp.int32) < lax.dynamic_index_in_dim(counts, shard, 0, False)
    positions = jnp.arange(pos_dev, dtype=jnp.int32)
    named = own_slots[:, None] == positions[None, :]
    picked = dot(named.astype(BF16), states).astype(BF16)
    left, right = shift(picked, "exp", 1), shift(picked, "exp", -1)
    half = slots // 2
    far_top, far_bottom = shift(left[:half], "exp", 1), shift(right[half:], "exp", -1)
    attn_gain, *swapped = lax.optimization_barrier((attn_gain, *swapped))
    *sent, base = project(
        info,
        (picked, left, right, far_top, far_bottom),
        attn_gain[None],
        query_weight,
        key_weight,
        value_weight,
    )

    base, out_part = lax.optimization_barrier((base, out_part))
    out_whole = lax.all_gather(out_part, ("dp", "core"), axis=0)

    mine = [sent[0]] + [shift(sent[k], "z", k) for k in range(1, RING)]
    theirs = [swap(piece) for piece in mine]
    attended = attend(info, mine, theirs)
    spread = lax.all_to_all(
        attended.reshape(RING * RING, ROW, HEAD),
        ("z", "exp"),
        split_axis=0,
        concat_axis=0,
        tiled=True,
    )
    hidden, normed = mix(spread, out_whole, base, moe_gain[None])

    table = jnp.stack(ring_all(table, "z"))
    table = jnp.stack([table[-dz % RING, -dy % RING] for dy, dz in OFFSETS])
    offsets_y = jnp.array([o[0] for o in OFFSETS], jnp.int32)
    offsets_z = jnp.array([o[1] for o in OFFSETS], jnp.int32)
    from_y, from_z = (y + offsets_y) % RING, (z + offsets_z) % RING
    top = routes.shape[1]
    experts_of = jnp.stack([(2 * z + core) * RING + y, (2 * z + 1 - core) * RING + y]).astype(F32)
    match = table[:, None, :, :top] == experts_of[None, :, None, None]
    row_ids = from_y[:, None] * ROW + jnp.arange(ROW, dtype=jnp.int32)[None, :]
    row_live = row_ids < counts[2 * from_z + core][:, None]
    taken = (jnp.any(match, axis=3) & row_live[:, None]).astype(jnp.int32)
    order = jnp.cumsum(taken, axis=2)
    rank = jnp.where(taken > 0, order - 1, -1)
    share = jnp.sum(jnp.where(match, table[:, None, :, top:], 0.0), axis=3)
    filled = ((order[:, :, -1] + 15) // 16 * 16).T
    ends = jnp.cumsum(filled, axis=1)
    region = jnp.array([[0], [REGION]], jnp.int32)
    segments = jnp.concatenate([(ends - filled + region).reshape(-1), (ends + region)[:, -1]])
    places = jnp.arange(2 * MOST, dtype=jnp.int32)
    second = places >= MOST
    seat = places - jnp.where(second, MOST, 0)
    sides = jnp.where(second[None, :, None], rank[:, 1, None, :], rank[:, 0, None, :])
    shares = jnp.where(second[None, :, None], share[:, 1, None, :], share[:, 0, None, :])
    hit = sides == seat[None, :, None]
    pick = hit.astype(BF16)
    worth = jnp.sum(jnp.where(hit, shares, 0.0), axis=2, keepdims=True)
    worth = jnp.broadcast_to(worth, (len(OFFSETS), 2 * MOST, ROW))
    sides = jnp.where(second[None, None, :], rank[:, 1, :, None], rank[:, 0, :, None])
    back = (sides == seat[None, None, :]).astype(BF16)

    made = experts(segments, pick, back, worth, collect(normed), weights + swapped)
    merged = (hidden.astype(F32) + give_back(made)).astype(BF16)
    spread = lax.all_to_all(merged, "exp", split_axis=1, concat_axis=0, tiled=True)
    here = (positions[:, None] == own_slots[None, :]) & live[None, :]
    placed = dot(here.astype(BF16), spread).astype(BF16)
    return jnp.where(jnp.any(here, axis=1)[:, None], placed, states)


def solution(mesh):
    dp, ctx, exp = (mesh.shape[axis] for axis in ("dp", "ctx", "exp"))
    cut = Mesh(mesh.devices.reshape(dp, ctx // 2, 2, exp), ("dp", "z", "core", "exp"))
    ctx_axes = ("z", "core")
    placed = (
        P(("dp", *ctx_axes), "exp"),
        P("dp"),
        P("dp"),
        P(),
        P(None, "exp"),
        P(None, "exp"),
        P(None, "exp"),
        P("exp", None),
        P(),
        P(("dp", *ctx_axes, "exp"), None),
        P(("dp", *ctx_axes, "exp"), None),
        P((*ctx_axes, "exp"), None, None),
        P((*ctx_axes, "exp"), None, None),
        P((*ctx_axes, "exp"), None, None),
    )
    return jax.shard_map(
        on_device,
        mesh=cut,
        in_specs=placed,
        out_specs=P(("dp", *ctx_axes), "exp"),
        check_vma=False,
    )
```

```python
import functools
import math

import jax
import jax.numpy as jnp
from jax import lax
from jax.experimental import pallas as pl
from jax.experimental.pallas import tpu as pltpu
from jax.sharding import Mesh, PartitionSpec as P

HEAD = 128
ROW = 128
HALF = 64
MOST = 48
UNIT = 256
WINDOW = 2 * MOST
SEATS = 2 * WINDOW
NOTE_LANES = 256
TILE = 256
REGION = 1920
EPS = 1e-05
RING = 4
F32 = jnp.float32
BF16 = jnp.bfloat16
AROUND = (0, -1, 1, 2)
PIECES = (4, 4, 4, 2, 2) * 2
HBM = pl.BlockSpec(memory_space=pl.ANY)
VMEM = pl.BlockSpec(memory_space=pltpu.VMEM)
SMEM = pl.BlockSpec(memory_space=pltpu.SMEM)


def dot(left, right):
    return jnp.dot(left, right, preferred_element_type=F32)


def shift(value, axis, step):
    return lax.ppermute(value, axis, [(i, (i + step) % RING) for i in range(RING)])


def ring_all(value, axis):
    return [value] + [shift(value, axis, step) for step in range(1, RING)]


def swap(value):
    return lax.ppermute(value, "core", [(0, 1), (1, 0)])


def rms(wide, gain):
    factor = lax.rsqrt(jnp.mean(wide * wide, axis=-1, keepdims=True) + EPS)
    return (wide * factor * gain).astype(BF16)


def project_kernel(info, own, left, right, far_top, far_bottom, gain, wq, wk, wv, *rest):
    outs, base, rows, normed, weights, made, sems = (
        rest[:4],
        rest[4],
        rest[5],
        rest[6],
        rest[7],
        rest[8],
        rest[9],
    )
    z, y = info[0], info[1]
    slots = normed.shape[0]
    top, bottom = far_top.shape[0], far_bottom.shape[0]
    part = own.shape[1]

    def columns(step):
        return pl.ds(pl.multiple_of(lax.rem(y + step, RING) * part, part), part)

    copies = [
        pltpu.make_async_copy(own, rows.at[:, columns(0)], sems.at[0]),
        pltpu.make_async_copy(left, rows.at[:, columns(3)], sems.at[1]),
        pltpu.make_async_copy(right, rows.at[:, columns(1)], sems.at[2]),
        pltpu.make_async_copy(far_top, rows.at[pl.ds(0, top), columns(2)], sems.at[3]),
        pltpu.make_async_copy(far_bottom, rows.at[pl.ds(top, bottom), columns(2)], sems.at[4]),
    ]
    loads = [
        pltpu.make_async_copy(w, weights.at[i], sems.at[5 + i]) for i, w in enumerate((wq, wk, wv))
    ]
    for copy in copies + loads:
        copy.start()
    for copy in copies:
        copy.wait()

    def norm(step, _):
        at = pl.ds(pl.multiple_of(step * 64, 64), 64)
        normed[at, :] = rms(rows[at, :].astype(F32), gain[...])
        return 0

    lax.fori_loop(0, slots // 64, norm, 0)
    base[...] = rows[pl.ds(pl.multiple_of(y * ROW, ROW), ROW), :]
    for i in range(3):
        loads[i].wait()

        def chunk(step, _, i=i):
            at = pl.ds(pl.multiple_of(step * 256, 256), 256)
            made[at, :] = dot(normed[at, :], weights[i]).astype(BF16)
            return 0

        lax.fori_loop(0, slots // 256, chunk, 0)
        for step, out in enumerate(outs):
            head = lax.rem(z + step, RING)
            out[0:slots, i * HEAD : (i + 1) * HEAD] = made[
                :, pl.ds(pl.multiple_of(head * HEAD, HEAD), HEAD)
            ]
    if rows.shape[0] > slots:
        lines = rows.shape[0] - slots
        for spot in range(RING * NOTE_LANES // HEAD):
            device, lane = divmod(spot * HEAD, NOTE_LANES)
            note = rows[slots:, device * part + lane : device * part + lane + HEAD]
            line, column = slots + spot // 3 * lines, spot % 3 * HEAD
            for out in outs:
                out[line : line + lines, column : column + HEAD] = note


def project(info, pieces, gain, wq, wk, wv):
    lines, part = pieces[0].shape
    slots = lines // (2 * ROW) * (2 * ROW)
    longer = slots + -(-RING * NOTE_LANES // (3 * HEAD)) * (lines - slots)
    width = gain.shape[-1]
    return pl.pallas_call(
        project_kernel,
        out_shape=[jax.ShapeDtypeStruct((longer, 3 * HEAD), BF16)] * RING
        + [jax.ShapeDtypeStruct((ROW, width), BF16)],
        in_specs=[SMEM] + [HBM] * 5 + [VMEM] + [HBM] * 3,
        out_specs=[VMEM] * 5,
        scratch_shapes=[
            pltpu.VMEM((lines, width), BF16),
            pltpu.VMEM((slots, width), BF16),
            pltpu.VMEM((3, width, part), BF16),
            pltpu.VMEM((slots, part), BF16),
            pltpu.SemaphoreType.DMA((8,)),
        ],
        compiler_params=pltpu.CompilerParams(vmem_limit_bytes=56 * 2**20),
        cost_estimate=pl.CostEstimate(
            flops=6 * slots * width * part, bytes_accessed=12 * 2**20, transcendentals=0
        ),
        name="project",
    )(info, *pieces, gain, wq, wk, wv)


def attend_kernel(info, *rest):
    mine, theirs, (out, held, sems) = rest[:RING], rest[RING : 2 * RING], rest[2 * RING :]
    z, core = info[0], info[2]
    slots = held.shape[1]
    half = slots // 2
    scale = math.log2(math.e) / HEAD**0.5
    copies = []
    for step in range(RING):
        chip = lax.rem(z + RING - step, RING)
        for source, shard in ((mine[step], 2 * chip + core), (theirs[step], 2 * chip + 1 - core)):
            source = source.at[pl.ds(0, slots), :]
            copies.append(pltpu.make_async_copy(source, held.at[shard], sems.at[len(copies)]))
    for copy in copies:
        copy.start()
    for copy in copies:
        copy.wait()

    def fold(carry, query, shard, keys, seen):
        top, mass, total = carry
        scores = (
            lax.dot_general(
                query,
                held[shard, keys, HEAD : 2 * HEAD],
                (((1,), (1,)), ((), ())),
                preferred_element_type=F32,
            )
            * scale
        )
        scores = seen(scores)
        top_new = jnp.maximum(top, jnp.max(scores, axis=1, keepdims=True))
        weights = jnp.exp2(scores - top_new)
        shrink = jnp.exp2(top - top_new)
        mass = mass * shrink + jnp.sum(weights, axis=1, keepdims=True)
        total = total * shrink + dot(weights.astype(BF16), held[shard, keys, 2 * HEAD :])
        return top_new, mass, total

    def tile(chip, own, rows):
        query = held[own, 0:rows, 0:HEAD]
        if rows < slots:
            out[chip, rows:, :] = jnp.zeros((slots - rows, HEAD), BF16)
        slot = lax.broadcasted_iota(jnp.int32, (rows, rows), 1)
        place = lax.broadcasted_iota(jnp.int32, (rows, rows), 0)
        mask = (slot <= place) & (slot < info[3 + own])
        carry = (
            jnp.full((rows, 1), -1e30, F32),
            jnp.zeros((rows, 1), F32),
            jnp.zeros((rows, HEAD), F32),
        )
        carry = fold(
            carry, query, own, slice(0, rows), lambda scores: jnp.where(mask, scores, -1e30)
        )

        def earlier(shard, state):
            slot = lax.broadcasted_iota(jnp.int32, (1, slots), 1)
            bias = jnp.where(slot < info[3 + shard], 0.0, -1e30)
            return fold(state, query, shard, slice(0, slots), lambda scores: scores + bias)

        top, mass, total = lax.fori_loop(0, own, earlier, carry)
        out[chip, 0:rows, :] = (total / mass).astype(BF16)

    def shard(chip, _):
        own = 2 * chip + core
        live = info[3 + own]

        cut = (half + slots) // 2

        @pl.when(live > cut)
        def _():
            tile(chip, own, slots)

        @pl.when((live > half) & (live <= cut))
        def _():
            tile(chip, own, cut)

        @pl.when(live <= half)
        def _():
            tile(chip, own, half)

        return 0

    lax.fori_loop(0, RING, shard, 0)


def attend(info, mine, theirs, slots):
    return pl.pallas_call(
        attend_kernel,
        out_shape=jax.ShapeDtypeStruct((RING, slots, HEAD), BF16),
        in_specs=[SMEM] + [HBM] * (len(mine) + len(theirs)),
        out_specs=VMEM,
        scratch_shapes=[
            pltpu.VMEM((2 * RING, slots, 3 * HEAD), BF16),
            pltpu.SemaphoreType.DMA((2 * RING,)),
        ],
        compiler_params=pltpu.CompilerParams(vmem_limit_bytes=56 * 2**20),
        cost_estimate=pl.CostEstimate(
            flops=20 * slots * slots * 4 * HEAD,
            bytes_accessed=4 * 2**20,
            transcendentals=20 * slots * slots,
        ),
        name="attend",
    )(info, *mine, *theirs)


def tabulate_kernel(info, *rest):
    sources, (pick, worth, segments, notes, taken, share, sems) = rest[: 2 * RING], rest[2 * RING :]
    z, y, core = info[0], info[1], info[2]
    units = pick.shape[0]
    lines = notes.shape[2]
    copies = [
        pltpu.make_async_copy(
            source.at[pl.ds(source.shape[0] - lines, lines), :],
            notes.at[i // RING, i % RING],
            sems.at[i],
        )
        for i, source in enumerate(sources)
    ]
    for copy in copies:
        copy.start()
    for copy in copies:
        copy.wait()
    lane = lax.broadcasted_iota(jnp.int32, (1, ROW), 1)
    named = [((2 * z + core) * RING + y), ((2 * z + 1 - core) * RING + y)]

    def block(index):
        side, far, near = index // 16, index // 4 % 4, index % 4
        far, near = AROUND[far] % RING, AROUND[near] % RING
        from_z = lax.rem(z + jnp.where(core == 0, far, near), RING)
        from_y = lax.rem(y + jnp.where(core == 0, near, far), RING)
        back = lax.rem(z + RING - from_z, RING)
        tiles = []
        for tile in range(2):
            spot = 2 * from_y + tile
            at = pl.ds(pl.multiple_of(spot // 3 * 16, 16), 16)
            column = pl.ds(pl.multiple_of(lax.rem(spot, 3) * HEAD, HEAD), HEAD)
            tiles.append(notes[side, back, at, column].astype(F32))
        half = lax.rem(core + from_y + from_z, 2)
        owner = 2 * from_z + (core if side == 0 else 1 - core)
        left = info[3 + owner] - from_y * ROW - half * HALF
        gates = tiles[0][8:] + (tiles[1][:8] + tiles[1][8:])
        return tiles[0][:8], gates, half, left

    for unit in range(units):
        for group in range(UNIT // ROW):
            index = 2 * (unit * (UNIT // ROW) + group)
            pair = [block(index), block(index + 1)]
            joined = []
            for part in range(2):
                first, second = (
                    jnp.where(half == at, values, pltpu.roll(values, HALF, 1))
                    for at, (values, half) in enumerate((b[part], b[2]) for b in pair)
                )
                joined.append(jnp.where(lane < HALF, first, second))
            left = jnp.where(lane < HALF, pair[0][3], pair[1][3] + HALF)
            live = jnp.where(lane < left, 1.0, 0.0)
            columns = slice(group * ROW, (group + 1) * ROW)
            for q in range(2):
                match = joined[0] == named[q].astype(F32)
                row = q * units + unit
                found = jnp.max(jnp.where(match, 1.0, 0.0), axis=0, keepdims=True)
                taken[row : row + 1, columns] = found * live
                share[row : row + 1, columns] = jnp.sum(
                    jnp.where(match, joined[1], 0.0), axis=0, keepdims=True
                )
    was = taken[...].astype(BF16)
    before = lax.broadcasted_iota(jnp.int32, (UNIT, UNIT), 0)
    after = lax.broadcasted_iota(jnp.int32, (UNIT, UNIT), 1)
    order = dot(was, (before <= after).astype(BF16))
    count = dot(was, jnp.ones((UNIT, ROW), BF16))
    filled = jnp.floor((count + 15.0) * 0.0625) * 16.0
    row = lax.broadcasted_iota(jnp.int32, (segments.shape[0], 2 * units), 0)
    other = lax.broadcasted_iota(jnp.int32, (segments.shape[0], 2 * units), 1)
    ends = row - 2 * units
    group = jnp.where(ends < 0, jnp.where(row < units, 0, 1), ends)
    same = jnp.where(other < units, 0, 1) == group
    sums = dot((same & ((ends >= 0) | (other < row))).astype(BF16), filled.astype(BF16))
    segments[...] = sums.astype(jnp.int32) + group[:, 0:1] * REGION
    taken[...] = jnp.where(taken[...] > 0.0, order - 1.0, -1.0)
    seat = lax.broadcasted_iota(jnp.int32, (WINDOW, UNIT), 0).astype(F32)
    for unit in range(units):
        for part in range(4):
            row = part % 2 * units + unit
            hit = seat + float(part // 2 * WINDOW) == taken[row : row + 1, :]
            at = slice(part * WINDOW, (part + 1) * WINDOW)
            pick[unit, at, :] = hit.astype(F32).astype(BF16)
            value = jnp.sum(jnp.where(hit, share[row : row + 1, :], 0.0), axis=1, keepdims=True)
            worth[unit, at, :] = jnp.broadcast_to(value, (WINDOW, ROW))


def tabulate(info, mine, theirs, slots):
    units = 2 * RING * RING * HALF // UNIT
    sources = list(mine) + list(theirs)
    lines = sources[0].shape[0] - slots
    return pl.pallas_call(
        tabulate_kernel,
        out_shape=[
            jax.ShapeDtypeStruct((units, 2 * SEATS, UNIT), BF16),
            jax.ShapeDtypeStruct((units, 2 * SEATS, ROW), F32),
            jax.ShapeDtypeStruct((2 * units + 8, ROW), jnp.int32),
        ],
        in_specs=[SMEM] + [HBM] * len(sources),
        out_specs=[VMEM] * 3,
        scratch_shapes=[
            pltpu.VMEM((2, RING, lines, 3 * HEAD), BF16),
            pltpu.VMEM((2 * units, UNIT), F32),
            pltpu.VMEM((2 * units, UNIT), F32),
            pltpu.SemaphoreType.DMA((2 * RING,)),
        ],
        compiler_params=pltpu.CompilerParams(vmem_limit_bytes=56 * 2**20),
        cost_estimate=pl.CostEstimate(flops=2**20, bytes_accessed=4 * 2**20, transcendentals=0),
        name="tabulate",
    )(info, *sources)


def mix_kernel(
    info, pieces, base, gain, mine, theirs, kept_hidden, lent_hidden, kept, lent, heads, total, held, sems
):
    parts, _, width = mine.shape
    core = info[2]
    copies = [
        pltpu.make_async_copy(weight.at[i], held.at[side, i], sems.at[side, i])
        for side, weight in enumerate((mine, theirs))
        for i in range(parts)
    ]
    for copy in copies:
        copy.start()
    for z in range(RING):
        for y in range(RING):
            at = (y * RING + z) * HEAD
            heads[:, at : at + HEAD] = pieces[z * RING + y]
    for i, copy in enumerate(copies):
        copy.wait()
        side, part = divmod(i, parts)
        column = 2 * part + (core if side == 0 else 1 - core)
        at = pl.ds(pl.multiple_of(column * width, width), width)
        total[:, at] = base[:, at].astype(F32) + dot(heads[...], held[side, part])
    keep = lax.rem(info[0] + info[1] + core, 2)
    for first, hidden, normed in ((keep, kept_hidden, kept), (1 - keep, lent_hidden, lent)):
        at = pl.ds(pl.multiple_of(first * HALF, HALF), HALF)
        made = total[at, :].astype(BF16)
        hidden[...] = made
        normed[...] = rms(made.astype(F32), gain[...])


def mix(info, pieces, mine, theirs, base, gain):
    parts, depth, width = mine.shape
    whole = 2 * parts * width
    return pl.pallas_call(
        mix_kernel,
        out_shape=[jax.ShapeDtypeStruct((HALF, whole), BF16)] * 4,
        in_specs=[SMEM, VMEM, VMEM, VMEM, HBM, HBM],
        out_specs=[VMEM] * 4,
        scratch_shapes=[
            pltpu.VMEM((ROW, depth), BF16),
            pltpu.VMEM((ROW, whole), F32),
            pltpu.VMEM((2, parts, depth, width), BF16),
            pltpu.SemaphoreType.DMA((2, parts)),
        ],
        compiler_params=pltpu.CompilerParams(vmem_limit_bytes=56 * 2**20),
        cost_estimate=pl.CostEstimate(
            flops=2 * ROW * depth * whole, bytes_accessed=10 * 2**20, transcendentals=0
        ),
        name="mix",
    )(info, pieces, base, gain, mine, theirs)


def expert_kernel(segments, pick, worth, *rest):
    count = len(PIECES)
    tokens, rest = rest[:count], rest[count:]
    weights, rest = rest[:6], rest[6:]
    outs, rest = rest[:count], rest[count:]
    held, chosen, act, scale, gates, ups, downs, token_sems, weight_sems, out_sems = rest
    units = held.shape[0] // UNIT
    width = held.shape[1]
    ff = act.shape[1]

    arriving, leaving, first = [], [], 0
    for i, piece in enumerate(PIECES):
        here = held.at[pl.ds(first * HALF, piece * HALF), :]
        arriving.append(pltpu.make_async_copy(tokens[i], here, token_sems.at[i]))
        leaving.append((first * HALF, piece * HALF))
        first += piece
        arriving[-1].start()
    parts = []
    for i, (chunk, at, rows, put) in enumerate(
        (chunk, *part)
        for chunk in range(2)
        for part in (
            (0, 256, (0, 0)),
            (256, 128, (3, 0)),
            (384, 128, (1, 128)),
            (512, 128, (2, 128)),
            (640, 128, (4, 0)),
            (768, 128, (1, 0)),
            (896, 128, (2, 0)),
        )
    ):
        here = held.at[pl.ds(chunk * 1024 + at, rows), :]
        there = outs[chunk * 5 + put[0]].at[pl.ds(put[1], rows), :]
        parts.append((chunk * 1024 + at + rows, pltpu.make_async_copy(here, there, out_sems.at[i])))
    loads = []
    for q in range(2):
        for i, place in enumerate((gates, ups, downs)):
            loads.append(
                pltpu.make_async_copy(
                    weights[3 * q + i].at[0], place.at[q], weight_sems.at[3 * q + i]
                )
            )

    def places(unit):
        return [pl.multiple_of(segments[q * units + unit], 16) for q in range(2)]

    def crowded(unit):
        ends = [segments[q * units + unit + 1] for q in range(2)]
        if unit == units - 1:
            ends = [segments[2 * units + q] for q in range(2)]
        used = [end - segments[q * units + unit] for q, end in enumerate(ends)]
        return jnp.maximum(used[0], used[1]) > WINDOW

    ready = 0
    for j in range(units):
        while ready < count and leaving[ready][0] < (j + 1) * UNIT:
            arriving[ready].wait()
            ready += 1
            if ready == count - 5:
                for copy in loads[:3]:
                    copy.start()
            elif ready == count:
                for copy in loads[3:]:
                    copy.start()
        starts = places(j)

        def gather(late, j=j, starts=starts):
            for q in range(2):
                at = pl.ds(starts[q] + late * WINDOW, WINDOW)
                scale[at, :] = worth[j, (2 * late + q) * WINDOW : (2 * late + q + 1) * WINDOW, :]
            for cut in range(width // 512):
                columns = slice(cut * 512, (cut + 1) * 512)
                sel = pick[j, late * SEATS : (late + 1) * SEATS, :]
                got = dot(sel, held[j * UNIT : (j + 1) * UNIT, columns]).astype(BF16)
                for q in range(2):
                    at = pl.ds(starts[q] + late * WINDOW, WINDOW)
                    chosen[at, columns] = got[q * WINDOW : (q + 1) * WINDOW]

        gather(0)
        pl.when(crowded(j))(functools.partial(gather, 1))
    for q in range(2):
        end = pl.multiple_of(segments[2 * units + q], 16)
        chosen[pl.ds(end, TILE + WINDOW), :] = jnp.zeros((TILE + WINDOW, width), BF16)
        scale[pl.ds(end, TILE + WINDOW), :] = jnp.zeros((TILE + WINDOW, ROW), F32)

    for q in range(2):
        for copy in loads[3 * q : 3 * q + 3]:
            copy.wait()

        def tile(start, rows, q=q):
            at = pl.ds(pl.multiple_of(q * REGION + start, 64), rows)
            for f in range(ff // 256):
                columns = slice(f * 256, (f + 1) * 256)
                x = chosen[at, :]
                gate = dot(x, gates[q, :, columns])
                up = dot(x, ups[q, :, columns])
                act[:rows, columns] = (gate / (1.0 + jnp.exp(-gate)) * up).astype(BF16)
            for f in range(width // 512):
                columns = slice(f * 512, (f + 1) * 512)
                made = dot(act[:rows, :], downs[q, :, columns])
                chosen[at, columns] = (made * scale[at, 0:1]).astype(BF16)

        def whole(t, _):
            tile(t * TILE, TILE)
            return 0

        used = segments[2 * units + q] - q * REGION
        full = lax.div(used + TILE // 2 - 1, TILE)
        lax.fori_loop(0, full, whole, 0)

        @pl.when(used > full * TILE)
        def _():
            tile(full * TILE, TILE // 2)

    for j in range(units):
        starts = places(j)

        def combine(seats, j=j, starts=starts):
            ats = [at + late for late in range(0, seats // 2, WINDOW) for at in starts]
            for cut in range(width // 512):
                columns = slice(cut * 512, (cut + 1) * 512)
                made = jnp.concatenate([chosen[pl.ds(at, WINDOW), columns] for at in ats], axis=0)
                sums = lax.dot_general(
                    pick[j, 0:seats, :],
                    made,
                    (((0,), (0,)), ((), ())),
                    preferred_element_type=F32,
                )
                held[j * UNIT : (j + 1) * UNIT, columns] = sums.astype(BF16)

        many = crowded(j)
        pl.when(many)(functools.partial(combine, 2 * SEATS))
        pl.when(jnp.logical_not(many))(functools.partial(combine, SEATS))
        for end, copy in parts:
            if j * UNIT < end <= (j + 1) * UNIT:
                copy.start()
    for _, copy in parts:
        copy.wait()


def experts(segments, pick, worth, pieces, weights):
    width = pieces[0].shape[1]
    ff = weights[0].shape[2]
    return pl.pallas_call(
        expert_kernel,
        out_shape=[jax.ShapeDtypeStruct((rows, width), BF16) for rows in (256, 256, 256, 128, 128) * 2],
        in_specs=[SMEM, VMEM, VMEM] + [HBM] * (len(pieces) + 6),
        out_specs=[HBM] * len(pieces),
        scratch_shapes=[
            pltpu.VMEM((sum(PIECES) * HALF, width), BF16),
            pltpu.VMEM((2 * REGION, width), BF16),
            pltpu.VMEM((TILE, ff), BF16),
            pltpu.VMEM((2 * REGION, ROW), F32),
            pltpu.VMEM((2, width, ff), BF16),
            pltpu.VMEM((2, width, ff), BF16),
            pltpu.VMEM((2, ff, width), BF16),
            pltpu.SemaphoreType.DMA((len(PIECES),)),
            pltpu.SemaphoreType.DMA((6,)),
            pltpu.SemaphoreType.DMA((14,)),
        ],
        compiler_params=pltpu.CompilerParams(vmem_limit_bytes=60 * 2**20),
        cost_estimate=pl.CostEstimate(
            flops=2 * 1024 * width * ff * 3, bytes_accessed=42 * 2**20, transcendentals=2**20
        ),
        name="experts",
    )(segments, pick, worth, *pieces, *weights)


def turn(value, phase, step):
    pairs = []
    for z in range(RING):
        for core in range(2):
            for y in range(RING):
                to_z, to_y = z, y
                if (phase + core) % 2 == 0:
                    to_y = (y + step) % RING
                else:
                    to_z = (z + step) % RING
                pairs.append(((z * 2 + core) * RING + y, (to_z * 2 + core) * RING + to_y))
    return lax.ppermute(value, ("z", "core", "exp"), pairs)


def ring_gather(own, phase):
    half = own.shape[0] // 2
    before, after = turn(own, phase, 1), turn(own, phase, -1)
    return [own, before, after, turn(before[:half], phase, 1), turn(after[half:], phase, -1)]


def add(first, *others):
    total = first.astype(F32)
    for other in others:
        total = total + other.astype(F32)
    return total.astype(BF16)


def collect(own):
    near = [own, turn(own, 0, 1), turn(own, 0, -1), turn(own, 0, 2)]
    return ring_gather(jnp.concatenate(near, axis=0), 1)


def give_back(chunks):
    first = [(turn(chunk[1], 1, -1), turn(chunk[2], 1, 1)) for chunk in chunks]
    sums = []
    for chunk, (back, ahead) in zip(chunks, first):
        half = back.shape[0] // 2
        top = turn(add(chunk[3], back[:half]), 1, -1)
        bottom = turn(add(chunk[4], ahead[:half]), 1, 1)
        upper = add(chunk[0][:half], ahead[half:], top)
        lower = add(chunk[0][half:], back[half:], bottom)
        cut = half // 2
        sums.append(
            (
                upper[:cut],
                turn(upper[cut:], 0, -1),
                turn(lower[:cut], 0, 1),
                turn(lower[cut:], 0, 2),
            )
        )
    return sums


def on_device(
    states,
    chosen,
    counts,
    attn_gain,
    query_weight,
    key_weight,
    value_weight,
    out_weight,
    moe_gain,
    routes,
    gate_probs,
    w_gate,
    w_up,
    w_down,
):
    x, z = lax.axis_index("dp"), lax.axis_index("z")
    core, y = lax.axis_index("core"), lax.axis_index("exp")
    pos_dev, part = states.shape
    slots = chosen.shape[0] // (2 * RING)
    width = attn_gain.shape[0]
    shard = 2 * z + core
    info = jnp.concatenate([jnp.stack([z, y, core]), counts]).astype(jnp.int32)

    cut = width // 8
    out_part = lax.dynamic_slice_in_dim(out_weight, (2 * x + core) * cut, cut, 1)
    out_part = lax.all_gather(out_part, "exp", axis=0, tiled=True)

    own_slots = lax.dynamic_slice_in_dim(chosen, shard * slots, slots)
    live = jnp.arange(slots, dtype=jnp.int32) < lax.dynamic_index_in_dim(counts, shard, 0, False)
    positions = jnp.arange(pos_dev, dtype=jnp.int32)
    named = own_slots[:, None] == positions[None, :]
    picked = dot(named.astype(BF16), states).astype(BF16)
    parts, rest = [], gate_probs
    for _ in range(3):
        parts.append(lax.reduce_precision(rest, 8, 7))
        rest = rest - parts[-1]
    note = jnp.concatenate([routes.astype(F32)] + parts, axis=1).astype(BF16).T
    note = jnp.concatenate([note[:16], note[16:]], axis=1)
    note = jnp.pad(note, ((0, 0), (0, part - NOTE_LANES)))
    own = jnp.concatenate([picked, note], axis=0)
    left, right = shift(own, "exp", 1), shift(own, "exp", -1)
    split = slots // 2 + note.shape[0]
    around = [left, right, shift(left[:split], "exp", 1), shift(right[split:], "exp", -1)]
    *sent, base = project(
        info, [own] + around, attn_gain[None], query_weight, key_weight, value_weight
    )
    base, out_part = lax.optimization_barrier((base, out_part))
    out_mine = lax.all_gather(out_part, "dp", axis=0)
    mine = [sent[0]] + [shift(sent[k], "z", k) for k in range(1, RING)]
    mine = lax.optimization_barrier(mine)
    theirs = [swap(piece) for piece in mine]

    weights = (w_gate, w_up, w_down)
    theirs[-1], *weights = lax.optimization_barrier((theirs[-1], *weights))
    swapped = [swap(w) for w in weights]
    attended = attend(info, mine, theirs, slots)
    out_mine, attended = lax.optimization_barrier((out_mine, attended))
    out_theirs = swap(out_mine)
    pick, worth, segments = tabulate(info, mine, theirs, slots)
    spread = lax.all_to_all(
        attended.reshape(RING * RING, ROW, HEAD),
        ("z", "exp"),
        split_axis=0,
        concat_axis=0,
        tiled=True,
    )
    spread, pick, *swapped = lax.optimization_barrier((spread, pick, *swapped))
    kept_hidden, lent_hidden, kept, lent = mix(info, spread, out_mine, out_theirs, base, moe_gain[None])
    pieces = collect(kept) + collect(swap(lent))
    made = experts(segments[:, 0], pick, worth, pieces, list(weights) + swapped)
    count = len(made) // 2
    sums = give_back([made[:count], made[count:]])
    merged = [add(kept_hidden, *sums[0]), add(swap(lent_hidden), *sums[1])]
    merged = jnp.stack(
        [jnp.where(core == 0, *merged), jnp.where(core == 0, *merged[::-1])]
    ).reshape(2, HALF, RING, part)
    merged = jnp.transpose(merged, (0, 2, 1, 3)).reshape(2 * RING, HALF, part)
    spread = lax.all_to_all(merged, ("core", "exp"), split_axis=0, concat_axis=0, tiled=True)
    spread = spread.reshape(2, RING, HALF, part)
    sides = jnp.arange(2, dtype=jnp.int32)[:, None]
    halves = (sides + z + jnp.arange(RING, dtype=jnp.int32)[None, :]) % 2
    slots_of = jnp.where(live, own_slots, -1).reshape(RING, 2, HALF)
    slots_of = jnp.where(halves[..., None] == 0, slots_of[None, :, 0], slots_of[None, :, 1])
    slots_of = slots_of.reshape(-1)
    spread = spread.reshape(slots, part)
    here = positions[:, None] == slots_of[None, :]
    placed = dot(here.astype(BF16), spread).astype(BF16)
    return jnp.where(jnp.any(here, axis=1)[:, None], placed, states)


def solution(mesh):
    dp, ctx, exp = (mesh.shape[axis] for axis in ("dp", "ctx", "exp"))
    cut = Mesh(mesh.devices.reshape(dp, ctx // 2, 2, exp), ("dp", "z", "core", "exp"))
    ctx_axes = ("z", "core")
    placed = (
        P(("dp", *ctx_axes), "exp"),
        P("dp"),
        P("dp"),
        P(),
        P(None, "exp"),
        P(None, "exp"),
        P(None, "exp"),
        P("exp", None),
        P(),
        P(("dp", *ctx_axes, "exp"), None),
        P(("dp", *ctx_axes, "exp"), None),
        P((*ctx_axes, "exp"), None, None),
        P((*ctx_axes, "exp"), None, None),
        P((*ctx_axes, "exp"), None, None),
    )
    return jax.shard_map(
        on_device,
        mesh=cut,
        in_specs=placed,
        out_specs=P(("dp", *ctx_axes), "exp"),
        check_vma=False,
    )
```

```python
import functools
import math

import jax
import jax.numpy as jnp
from jax import lax
from jax.experimental import pallas as pl
from jax.experimental.pallas import tpu as pltpu
from jax.sharding import Mesh, PartitionSpec as P

HEAD = 128
ROW = 128
HALF = 64
MOST = 48
UNIT = 256
WINDOW = 2 * MOST
SEATS = 2 * WINDOW
NOTE_LANES = 256
TILE = 256
REGION = 1920
EPS = 1e-05
RING = 4
F32 = jnp.float32
BF16 = jnp.bfloat16
AROUND = (0, -1, 1, 2)
PIECES = (4, 4, 4, 2, 2) * 2
HBM = pl.BlockSpec(memory_space=pl.ANY)
VMEM = pl.BlockSpec(memory_space=pltpu.VMEM)
SMEM = pl.BlockSpec(memory_space=pltpu.SMEM)


def dot(left, right):
    return jnp.dot(left, right, preferred_element_type=F32)


def shift(value, axis, step):
    return lax.ppermute(value, axis, [(i, (i + step) % RING) for i in range(RING)])


def ring_all(value, axis):
    return [value] + [shift(value, axis, step) for step in range(1, RING)]


def swap(value):
    return lax.ppermute(value, "core", [(0, 1), (1, 0)])


def rms(wide, gain):
    factor = lax.rsqrt(jnp.mean(wide * wide, axis=-1, keepdims=True) + EPS)
    return (wide * factor * gain).astype(BF16)


def fetch_kernel(chosen, routes, gates, states, out, held, sems):
    count, slots = sems.shape[0], chosen.shape[1]
    rows, part = held.shape[0] // count, held.shape[1]
    copies = [
        pltpu.make_async_copy(
            states.at[pl.ds(i * rows, rows), :], held.at[pl.ds(i * rows, rows), :], sems.at[i]
        )
        for i in range(count)
    ]
    for copy in copies:
        copy.start()
    parts, rest = [routes[...].astype(F32)], gates[...]
    for _ in range(3):
        parts.append(rest.astype(BF16).astype(F32))
        rest = rest - parts[-1]
    out[slots:, :] = jnp.zeros((out.shape[0] - slots, part), BF16)
    for tile in range(2):
        pair = parts[2 * tile : 2 * tile + 2]
        out[slots:, tile * ROW : (tile + 1) * ROW] = jnp.concatenate(pair, axis=0).astype(BF16)
    mine = chosen[...]
    total = None
    for i, copy in enumerate(copies):
        place = lax.broadcasted_iota(jnp.int32, (rows, slots), 0) + i * rows
        named = (place == mine).astype(F32).astype(BF16)
        copy.wait()
        some = lax.dot_general(
            named,
            held[i * rows : (i + 1) * rows, :],
            (((0,), (0,)), ((), ())),
            preferred_element_type=F32,
        )
        total = some if total is None else total + some
    out[0:slots, :] = total.astype(BF16)


def fetch(chosen, routes, gates, states):
    slots, (positions, part) = chosen.shape[1], states.shape
    return pl.pallas_call(
        fetch_kernel,
        out_shape=jax.ShapeDtypeStruct((slots + 16, part), BF16),
        in_specs=[VMEM, VMEM, VMEM, HBM],
        out_specs=VMEM,
        scratch_shapes=[pltpu.VMEM((positions, part), BF16), pltpu.SemaphoreType.DMA((4,))],
        compiler_params=pltpu.CompilerParams(vmem_limit_bytes=56 * 2**20),
        cost_estimate=pl.CostEstimate(
            flops=2 * slots * positions * part, bytes_accessed=4 * 2**20, transcendentals=0
        ),
        name="fetch",
    )(chosen, routes, gates, states)


def project_kernel(info, own, left, right, far_top, far_bottom, gain, wq, wk, wv, *rest):
    outs, base, rows, normed, weights, made, sems = (
        rest[:4],
        rest[4],
        rest[5],
        rest[6],
        rest[7],
        rest[8],
        rest[9],
    )
    z, y = info[0], info[1]
    slots = normed.shape[0]
    top, bottom = far_top.shape[0], far_bottom.shape[0]
    part = own.shape[1]

    def columns(step):
        return pl.ds(pl.multiple_of(lax.rem(y + step, RING) * part, part), part)

    copies = [
        pltpu.make_async_copy(own, rows.at[:, columns(0)], sems.at[0]),
        pltpu.make_async_copy(left, rows.at[:, columns(3)], sems.at[1]),
        pltpu.make_async_copy(right, rows.at[:, columns(1)], sems.at[2]),
        pltpu.make_async_copy(far_top, rows.at[pl.ds(0, top), columns(2)], sems.at[3]),
        pltpu.make_async_copy(far_bottom, rows.at[pl.ds(top, bottom), columns(2)], sems.at[4]),
    ]
    loads = [
        pltpu.make_async_copy(w, weights.at[i], sems.at[5 + i]) for i, w in enumerate((wq, wk, wv))
    ]
    for copy in copies + loads:
        copy.start()
    for copy in copies:
        copy.wait()

    def norm(step, _):
        at = pl.ds(pl.multiple_of(step * 64, 64), 64)
        normed[at, :] = rms(rows[at, :].astype(F32), gain[...])
        return 0

    lax.fori_loop(0, slots // 64, norm, 0)
    base[...] = rows[pl.ds(pl.multiple_of(y * ROW, ROW), ROW), :]
    for i in range(3):
        loads[i].wait()

        def chunk(step, _, i=i):
            at = pl.ds(pl.multiple_of(step * 256, 256), 256)
            made[at, :] = dot(normed[at, :], weights[i]).astype(BF16)
            return 0

        lax.fori_loop(0, slots // 256, chunk, 0)
        for step, out in enumerate(outs):
            head = lax.rem(z + step, RING)
            out[0:slots, i * HEAD : (i + 1) * HEAD] = made[
                :, pl.ds(pl.multiple_of(head * HEAD, HEAD), HEAD)
            ]
    if rows.shape[0] > slots:
        lines = rows.shape[0] - slots
        for spot in range(RING * NOTE_LANES // HEAD):
            device, lane = divmod(spot * HEAD, NOTE_LANES)
            note = rows[slots:, device * part + lane : device * part + lane + HEAD]
            line, column = slots + spot // 3 * lines, spot % 3 * HEAD
            for out in outs:
                out[line : line + lines, column : column + HEAD] = note


def project(info, pieces, gain, wq, wk, wv):
    lines, part = pieces[0].shape
    slots = lines // (2 * ROW) * (2 * ROW)
    longer = slots + -(-RING * NOTE_LANES // (3 * HEAD)) * (lines - slots)
    width = gain.shape[-1]
    return pl.pallas_call(
        project_kernel,
        out_shape=[jax.ShapeDtypeStruct((longer, 3 * HEAD), BF16)] * RING
        + [jax.ShapeDtypeStruct((ROW, width), BF16)],
        in_specs=[SMEM] + [HBM] * 5 + [VMEM] + [HBM] * 3,
        out_specs=[VMEM] * 5,
        scratch_shapes=[
            pltpu.VMEM((lines, width), BF16),
            pltpu.VMEM((slots, width), BF16),
            pltpu.VMEM((3, width, part), BF16),
            pltpu.VMEM((slots, part), BF16),
            pltpu.SemaphoreType.DMA((8,)),
        ],
        compiler_params=pltpu.CompilerParams(vmem_limit_bytes=56 * 2**20),
        cost_estimate=pl.CostEstimate(
            flops=6 * slots * width * part, bytes_accessed=12 * 2**20, transcendentals=0
        ),
        name="project",
    )(info, *pieces, gain, wq, wk, wv)


def attend_kernel(info, *rest):
    mine, theirs, (out, held, sems) = rest[:RING], rest[RING : 2 * RING], rest[2 * RING :]
    z, core = info[0], info[2]
    slots = held.shape[1]
    half = slots // 2
    scale = math.log2(math.e) / HEAD**0.5
    copies = []
    for step in range(RING):
        chip = lax.rem(z + RING - step, RING)
        for source, shard in ((mine[step], 2 * chip + core), (theirs[step], 2 * chip + 1 - core)):
            source = source.at[pl.ds(0, slots), :]
            copies.append(pltpu.make_async_copy(source, held.at[shard], sems.at[len(copies)]))
    for copy in copies:
        copy.start()
    for copy in copies:
        copy.wait()

    def fold(carry, query, shard, keys, seen):
        top, mass, total = carry
        scores = (
            lax.dot_general(
                query,
                held[shard, keys, HEAD : 2 * HEAD],
                (((1,), (1,)), ((), ())),
                preferred_element_type=F32,
            )
            * scale
        )
        scores = seen(scores)
        top_new = jnp.maximum(top, jnp.max(scores, axis=1, keepdims=True))
        weights = jnp.exp2(scores - top_new)
        shrink = jnp.exp2(top - top_new)
        mass = mass * shrink + jnp.sum(weights, axis=1, keepdims=True)
        total = total * shrink + dot(weights.astype(BF16), held[shard, keys, 2 * HEAD :])
        return top_new, mass, total

    def tile(chip, own, rows):
        query = held[own, 0:rows, 0:HEAD]
        if rows < slots:
            out[chip, rows:, :] = jnp.zeros((slots - rows, HEAD), BF16)
        slot = lax.broadcasted_iota(jnp.int32, (rows, rows), 1)
        place = lax.broadcasted_iota(jnp.int32, (rows, rows), 0)
        mask = (slot <= place) & (slot < info[3 + own])
        carry = (
            jnp.full((rows, 1), -1e30, F32),
            jnp.zeros((rows, 1), F32),
            jnp.zeros((rows, HEAD), F32),
        )
        carry = fold(
            carry, query, own, slice(0, rows), lambda scores: jnp.where(mask, scores, -1e30)
        )

        def earlier(shard, state):
            slot = lax.broadcasted_iota(jnp.int32, (1, slots), 1)
            bias = jnp.where(slot < info[3 + shard], 0.0, -1e30)
            return fold(state, query, shard, slice(0, slots), lambda scores: scores + bias)

        top, mass, total = lax.fori_loop(0, own, earlier, carry)
        out[chip, 0:rows, :] = (total / mass).astype(BF16)

    def shard(chip, _):
        own = 2 * chip + core
        live = info[3 + own]

        cut = (half + slots) // 2

        @pl.when(live > cut)
        def _():
            tile(chip, own, slots)

        @pl.when((live > half) & (live <= cut))
        def _():
            tile(chip, own, cut)

        @pl.when(live <= half)
        def _():
            tile(chip, own, half)

        return 0

    lax.fori_loop(0, RING, shard, 0)


def attend(info, mine, theirs, slots):
    return pl.pallas_call(
        attend_kernel,
        out_shape=jax.ShapeDtypeStruct((RING, slots, HEAD), BF16),
        in_specs=[SMEM] + [HBM] * (len(mine) + len(theirs)),
        out_specs=VMEM,
        scratch_shapes=[
            pltpu.VMEM((2 * RING, slots, 3 * HEAD), BF16),
            pltpu.SemaphoreType.DMA((2 * RING,)),
        ],
        compiler_params=pltpu.CompilerParams(vmem_limit_bytes=56 * 2**20),
        cost_estimate=pl.CostEstimate(
            flops=20 * slots * slots * 4 * HEAD,
            bytes_accessed=4 * 2**20,
            transcendentals=20 * slots * slots,
        ),
        name="attend",
    )(info, *mine, *theirs)


def tabulate_kernel(info, *rest):
    sources, (pick, worth, segments, notes, taken, share, sems) = rest[: 2 * RING], rest[2 * RING :]
    z, y, core = info[0], info[1], info[2]
    units = pick.shape[0]
    lines = notes.shape[2]
    copies = [
        pltpu.make_async_copy(
            source.at[pl.ds(source.shape[0] - lines, lines), :],
            notes.at[i // RING, i % RING],
            sems.at[i],
        )
        for i, source in enumerate(sources)
    ]
    for copy in copies:
        copy.start()
    for copy in copies:
        copy.wait()
    lane = lax.broadcasted_iota(jnp.int32, (1, ROW), 1)
    named = [((2 * z + core) * RING + y), ((2 * z + 1 - core) * RING + y)]

    def block(index):
        side, far, near = index // 16, index // 4 % 4, index % 4
        far, near = AROUND[far] % RING, AROUND[near] % RING
        from_z = lax.rem(z + jnp.where(core == 0, far, near), RING)
        from_y = lax.rem(y + jnp.where(core == 0, near, far), RING)
        back = lax.rem(z + RING - from_z, RING)
        tiles = []
        for tile in range(2):
            spot = 2 * from_y + tile
            at = pl.ds(pl.multiple_of(spot // 3 * 16, 16), 16)
            column = pl.ds(pl.multiple_of(lax.rem(spot, 3) * HEAD, HEAD), HEAD)
            tiles.append(notes[side, back, at, column].astype(F32))
        half = lax.rem(core + from_y + from_z, 2)
        owner = 2 * from_z + (core if side == 0 else 1 - core)
        left = info[3 + owner] - from_y * ROW - half * HALF
        gates = tiles[0][8:] + (tiles[1][:8] + tiles[1][8:])
        return tiles[0][:8], gates, half, left

    for unit in range(units):
        for group in range(UNIT // ROW):
            index = 2 * (unit * (UNIT // ROW) + group)
            pair = [block(index), block(index + 1)]
            joined = []
            for part in range(2):
                first, second = (
                    jnp.where(half == at, values, pltpu.roll(values, HALF, 1))
                    for at, (values, half) in enumerate((b[part], b[2]) for b in pair)
                )
                joined.append(jnp.where(lane < HALF, first, second))
            left = jnp.where(lane < HALF, pair[0][3], pair[1][3] + HALF)
            live = jnp.where(lane < left, 1.0, 0.0)
            columns = slice(group * ROW, (group + 1) * ROW)
            for q in range(2):
                match = joined[0] == named[q].astype(F32)
                row = q * units + unit
                found = jnp.max(jnp.where(match, 1.0, 0.0), axis=0, keepdims=True)
                taken[row : row + 1, columns] = found * live
                share[row : row + 1, columns] = jnp.sum(
                    jnp.where(match, joined[1], 0.0), axis=0, keepdims=True
                )
    was = taken[...].astype(BF16)
    before = lax.broadcasted_iota(jnp.int32, (UNIT, UNIT), 0)
    after = lax.broadcasted_iota(jnp.int32, (UNIT, UNIT), 1)
    order = dot(was, (before <= after).astype(BF16))
    count = dot(was, jnp.ones((UNIT, ROW), BF16))
    filled = jnp.floor((count + 15.0) * 0.0625) * 16.0
    row = lax.broadcasted_iota(jnp.int32, (segments.shape[0], 2 * units), 0)
    other = lax.broadcasted_iota(jnp.int32, (segments.shape[0], 2 * units), 1)
    ends = row - 2 * units
    group = jnp.where(ends < 0, jnp.where(row < units, 0, 1), ends)
    same = jnp.where(other < units, 0, 1) == group
    sums = dot((same & ((ends >= 0) | (other < row))).astype(BF16), filled.astype(BF16))
    segments[...] = sums.astype(jnp.int32) + group[:, 0:1] * REGION
    taken[...] = jnp.where(taken[...] > 0.0, order - 1.0, -1.0)
    seat = lax.broadcasted_iota(jnp.int32, (WINDOW, UNIT), 0).astype(F32)
    for unit in range(units):
        for part in range(4):
            row = part % 2 * units + unit
            hit = seat + float(part // 2 * WINDOW) == taken[row : row + 1, :]
            at = slice(part * WINDOW, (part + 1) * WINDOW)
            pick[unit, at, :] = hit.astype(F32).astype(BF16)
            value = jnp.sum(jnp.where(hit, share[row : row + 1, :], 0.0), axis=1, keepdims=True)
            worth[unit, at, :] = jnp.broadcast_to(value, (WINDOW, ROW))


def tabulate(info, mine, theirs, slots):
    units = 2 * RING * RING * HALF // UNIT
    sources = list(mine) + list(theirs)
    lines = sources[0].shape[0] - slots
    return pl.pallas_call(
        tabulate_kernel,
        out_shape=[
            jax.ShapeDtypeStruct((units, 2 * SEATS, UNIT), BF16),
            jax.ShapeDtypeStruct((units, 2 * SEATS, ROW), F32),
            jax.ShapeDtypeStruct((2 * units + 8, ROW), jnp.int32),
        ],
        in_specs=[SMEM] + [HBM] * len(sources),
        out_specs=[VMEM] * 3,
        scratch_shapes=[
            pltpu.VMEM((2, RING, lines, 3 * HEAD), BF16),
            pltpu.VMEM((2 * units, UNIT), F32),
            pltpu.VMEM((2 * units, UNIT), F32),
            pltpu.SemaphoreType.DMA((2 * RING,)),
        ],
        compiler_params=pltpu.CompilerParams(vmem_limit_bytes=56 * 2**20),
        cost_estimate=pl.CostEstimate(flops=2**20, bytes_accessed=4 * 2**20, transcendentals=0),
        name="tabulate",
    )(info, *sources)


def mix_kernel(
    info, pieces, base, gain, mine, theirs, kept_hidden, lent_hidden, kept, lent, heads, total, held, sems
):
    parts, _, width = mine.shape
    core = info[2]
    copies = [
        pltpu.make_async_copy(weight.at[i], held.at[side, i], sems.at[side, i])
        for side, weight in enumerate((mine, theirs))
        for i in range(parts)
    ]
    for copy in copies:
        copy.start()
    for z in range(RING):
        for y in range(RING):
            at = (y * RING + z) * HEAD
            heads[:, at : at + HEAD] = pieces[z * RING + y]
    for i, copy in enumerate(copies):
        copy.wait()
        if i % 2 == 0:
            continue
        side, part = divmod(i, parts)
        made = [dot(heads[...], held[side, part - 1 + k]) for k in range(2)]
        for k in range(2):
            column = 2 * (part - 1 + k) + (core if side == 0 else 1 - core)
            at = pl.ds(pl.multiple_of(column * width, width), width)
            total[:, at] = base[:, at].astype(F32) + made[k]
    keep = lax.rem(info[0] + info[1] + core, 2)
    for first, hidden, normed in ((keep, kept_hidden, kept), (1 - keep, lent_hidden, lent)):
        at = pl.ds(pl.multiple_of(first * HALF, HALF), HALF)
        made = total[at, :].astype(BF16)
        hidden[...] = made
        normed[...] = rms(made.astype(F32), gain[...])


def mix(info, pieces, mine, theirs, base, gain):
    parts, depth, width = mine.shape
    whole = 2 * parts * width
    return pl.pallas_call(
        mix_kernel,
        out_shape=[jax.ShapeDtypeStruct((HALF, whole), BF16)] * 4,
        in_specs=[SMEM, VMEM, VMEM, VMEM, HBM, HBM],
        out_specs=[VMEM] * 4,
        scratch_shapes=[
            pltpu.VMEM((ROW, depth), BF16),
            pltpu.VMEM((ROW, whole), F32),
            pltpu.VMEM((2, parts, depth, width), BF16),
            pltpu.SemaphoreType.DMA((2, parts)),
        ],
        compiler_params=pltpu.CompilerParams(vmem_limit_bytes=56 * 2**20),
        cost_estimate=pl.CostEstimate(
            flops=2 * ROW * depth * whole, bytes_accessed=10 * 2**20, transcendentals=0
        ),
        name="mix",
    )(info, pieces, base, gain, mine, theirs)


def expert_kernel(info, segments, pick, worth, kept, lent, *rest):
    count = len(PIECES)
    tokens, rest = rest[:count], rest[count:]
    weights, rest = rest[:6], rest[6:]
    outs, rest = rest[:5], rest[5:]
    held, chosen, act, scale, gates, ups, downs, token_sems, weight_sems, out_sems = rest
    units = 2 * RING
    width = held.shape[-1]
    y, core = info[1], info[2]
    ff = act.shape[1]

    arriving = []
    for i, token in enumerate(tokens):
        chunk, piece = divmod(i, count // 2)
        here = held.at[chunk, piece] if piece < 3 else held.at[chunk, 3, pl.ds(2 * piece - 6, 2)]
        arriving.append(pltpu.make_async_copy(token, here, token_sems.at[i]))
        arriving[-1].start()

    def leaving(chunk, wide):
        own, back, ahead, late_back, late_ahead = outs
        places = (
            own.at[chunk],
            late_back if chunk == 0 else back.at[1],
            ahead.at[1] if chunk == 0 else late_ahead,
            back.at[0] if chunk == 0 else ahead.at[0],
        )
        copies = []
        for piece, place in enumerate(places):
            for block in range(RING):
                if wide:
                    columns = pl.ds(block * (width // RING), width // RING)
                    here = held.at[chunk, piece, :, :, columns]
                else:
                    which = lax.rem(y + AROUND[piece] % RING, RING)
                    step = width // RING
                    columns = pl.ds(pl.multiple_of(which * step, step), step)
                    here = held.at[chunk, :, block, :, columns]
                sem = out_sems.at[chunk, piece, block]
                copies.append(pltpu.make_async_copy(here, place.at[block], sem))
        return copies

    loads = []
    for q in range(2):
        for i, place in enumerate((gates, ups, downs)):
            loads.append(
                pltpu.make_async_copy(
                    weights[3 * q + i].at[0], place.at[q], weight_sems.at[3 * q + i]
                )
            )

    def places(unit):
        return [pl.multiple_of(segments[q * units + unit], 16) for q in range(2)]

    def crowded(unit):
        ends = [segments[q * units + unit + 1] for q in range(2)]
        if unit == units - 1:
            ends = [segments[2 * units + q] for q in range(2)]
        used = [end - segments[q * units + unit] for q, end in enumerate(ends)]
        return jnp.maximum(used[0], used[1]) > WINDOW

    ready = 0
    for j in range(units):
        while ready < count // 2 * (j // RING) + min(j % RING, 3) + (2 if j % RING == 3 else 1):
            arriving[ready].wait()
            ready += 1
            if ready == count - 5:
                for copy in loads[:3]:
                    copy.start()
            elif ready == count:
                for copy in loads[3:]:
                    copy.start()
        starts = places(j)

        def gather(late, j=j, starts=starts):
            for q in range(2):
                at = pl.ds(starts[q] + late * WINDOW, WINDOW)
                scale[at, :] = worth[j, (2 * late + q) * WINDOW : (2 * late + q + 1) * WINDOW, :]
            for cut in range(width // 512):
                columns = slice(cut * 512, (cut + 1) * 512)
                sel = pick[j, late * SEATS : (late + 1) * SEATS, :]
                got = dot(sel, held[j // RING, j % RING, :, :, columns].reshape(UNIT, 512)).astype(BF16)
                for q in range(2):
                    at = pl.ds(starts[q] + late * WINDOW, WINDOW)
                    chosen[at, columns] = got[q * WINDOW : (q + 1) * WINDOW]

        gather(0)
        pl.when(crowded(j))(functools.partial(gather, 1))
    for q in range(2):
        end = pl.multiple_of(segments[2 * units + q], 16)
        chosen[pl.ds(end, TILE + WINDOW), :] = jnp.zeros((TILE + WINDOW, width), BF16)
        scale[pl.ds(end, TILE + WINDOW), :] = jnp.zeros((TILE + WINDOW, ROW), F32)

    for q in range(2):
        for copy in loads[3 * q : 3 * q + 3]:
            copy.wait()

        def tile(start, rows, q=q):
            at = pl.ds(pl.multiple_of(q * REGION + start, 64), rows)
            for f in range(ff // 256):
                columns = slice(f * 256, (f + 1) * 256)
                x = chosen[at, :]
                gate = dot(x, gates[q, :, columns])
                up = dot(x, ups[q, :, columns])
                act[:rows, columns] = (gate / (1.0 + jnp.exp(-gate)) * up).astype(BF16)
            for f in range(width // 512):
                columns = slice(f * 512, (f + 1) * 512)
                made = dot(act[:rows, :], downs[q, :, columns])
                chosen[at, columns] = (made * scale[at, 0:1]).astype(BF16)

        def whole(t, _):
            tile(t * TILE, TILE)
            return 0

        used = segments[2 * units + q] - q * REGION
        full = lax.div(used + TILE // 2 - 1, TILE)
        lax.fori_loop(0, full, whole, 0)

        @pl.when(used > full * TILE)
        def _():
            tile(full * TILE, TILE // 2)

    for j in range(units):
        starts = places(j)

        def combine(seats, j=j, starts=starts):
            ats = [at + late for late in range(0, seats // 2, WINDOW) for at in starts]
            for cut in range(width // 512):
                columns = slice(cut * 512, (cut + 1) * 512)
                made = jnp.concatenate([chosen[pl.ds(at, WINDOW), columns] for at in ats], axis=0)
                sums = lax.dot_general(
                    pick[j, 0:seats, :],
                    made,
                    (((0,), (0,)), ((), ())),
                    preferred_element_type=F32,
                )
                if j % RING == 0:
                    hidden = (kept if j == 0 else lent)[:, columns].astype(F32)
                    sums = jnp.concatenate([sums[:HALF] + hidden, sums[HALF:]], axis=0)
                made = sums.astype(BF16).reshape(RING, HALF, 512)
                for block in range(RING):
                    at_y = [lax.rem(y + AROUND[i] % RING, RING) for i in (j % RING, block)]
                    first = jnp.where(core == 0, j % RING, at_y[0])
                    second = jnp.where(core == 0, at_y[1], block)
                    held[j // RING, first, second, :, columns] = made[block]

        many = crowded(j)
        pl.when(many)(functools.partial(combine, 2 * SEATS))
        pl.when(jnp.logical_not(many))(functools.partial(combine, SEATS))
        if j % RING == RING - 1:
            for wide in (True, False):

                @pl.when(core == (0 if wide else 1))
                def _(j=j, wide=wide):
                    for copy in leaving(j // RING, wide):
                        copy.start()

    for wide in (True, False):

        @pl.when(core == (0 if wide else 1))
        def _(wide=wide):
            for chunk in range(2):
                for copy in leaving(chunk, wide):
                    copy.wait()


def experts(info, segments, pick, worth, kept, lent, pieces, weights):
    width = pieces[0].shape[1]
    pieces = [piece.reshape(-1, HALF, width) for piece in pieces]
    block = (RING, RING, HALF, width // RING)
    ff = weights[0].shape[2]
    return pl.pallas_call(
        expert_kernel,
        out_shape=[jax.ShapeDtypeStruct((2, *block), BF16)] * 3 + [jax.ShapeDtypeStruct(block, BF16)] * 2,
        in_specs=[SMEM, SMEM, VMEM, VMEM, VMEM, VMEM] + [HBM] * (len(pieces) + 6),
        out_specs=[HBM] * 5,
        scratch_shapes=[
            pltpu.VMEM((2, RING, RING, HALF, width), BF16),
            pltpu.VMEM((2 * REGION, width), BF16),
            pltpu.VMEM((TILE, ff), BF16),
            pltpu.VMEM((2 * REGION, ROW), F32),
            pltpu.VMEM((2, width, ff), BF16),
            pltpu.VMEM((2, width, ff), BF16),
            pltpu.VMEM((2, ff, width), BF16),
            pltpu.SemaphoreType.DMA((len(PIECES),)),
            pltpu.SemaphoreType.DMA((6,)),
            pltpu.SemaphoreType.DMA((2, RING, RING)),
        ],
        compiler_params=pltpu.CompilerParams(vmem_limit_bytes=60 * 2**20),
        cost_estimate=pl.CostEstimate(
            flops=2 * 1024 * width * ff * 3, bytes_accessed=42 * 2**20, transcendentals=2**20
        ),
        name="experts",
    )(info, segments, pick, worth, kept, lent, *pieces, *weights)


def turn(value, phase, step):
    pairs = []
    for z in range(RING):
        for core in range(2):
            for y in range(RING):
                to_z, to_y = z, y
                if (phase + core) % 2 == 0:
                    to_y = (y + step) % RING
                else:
                    to_z = (z + step) % RING
                pairs.append(((z * 2 + core) * RING + y, (to_z * 2 + core) * RING + to_y))
    return lax.ppermute(value, ("z", "core", "exp"), pairs)


def ring_gather(own, phase):
    half = own.shape[0] // 2
    before, after = turn(own, phase, 1), turn(own, phase, -1)
    return [own, before, after, turn(before[:half], phase, 1), turn(after[half:], phase, -1)]


def add(first, *others):
    total = first.astype(F32)
    for other in others:
        total = total + other.astype(F32)
    return total.astype(BF16)


def collect(own):
    near = [own, turn(own, 0, 1), turn(own, 0, -1), turn(own, 0, 2)]
    return ring_gather(jnp.concatenate(near, axis=0), 1)


def give_back(pieces, y, core):
    own, back, ahead, late_back, late_ahead = pieces
    back, ahead = turn(back, 1, -1), turn(ahead, 1, 1)
    late_back = turn(add(late_back, back[0]), 1, -1)
    late_ahead = turn(add(late_ahead, ahead[0]), 1, 1)
    sums = ((own[0], ahead[1], late_back), (own[1], back[1], late_ahead))

    def block(index):
        at = jnp.where(core == 0, (y + AROUND[index]) % RING, index)
        return jnp.stack(
            [add(*(lax.dynamic_index_in_dim(s, at, 0, keepdims=False) for s in some)) for some in sums]
        )

    return add(block(0), turn(block(1), 0, -1), turn(block(2), 0, 1), turn(block(3), 0, 2))


def on_device(
    states,
    chosen,
    counts,
    attn_gain,
    query_weight,
    key_weight,
    value_weight,
    out_weight,
    moe_gain,
    routes,
    gate_probs,
    w_gate,
    w_up,
    w_down,
):
    x, z = lax.axis_index("dp"), lax.axis_index("z")
    core, y = lax.axis_index("core"), lax.axis_index("exp")
    pos_dev, part = states.shape
    slots = chosen.shape[0] // (2 * RING)
    width = attn_gain.shape[0]
    shard = 2 * z + core
    info = jnp.concatenate([jnp.stack([z, y, core]), counts]).astype(jnp.int32)

    own_slots = lax.dynamic_slice_in_dim(chosen, shard * slots, slots)
    live = jnp.arange(slots, dtype=jnp.int32) < lax.dynamic_index_in_dim(counts, shard, 0, False)
    positions = jnp.arange(pos_dev, dtype=jnp.int32)
    own = fetch(own_slots[None], routes.T, gate_probs.T, states)
    cut = width // 8
    own, out_weight = lax.optimization_barrier((own, out_weight))
    out_part = lax.dynamic_slice_in_dim(out_weight, (2 * x + core) * cut, cut, 1)
    out_part = lax.all_gather(out_part, "exp", axis=0, tiled=True)
    left, right = shift(own, "exp", 1), shift(own, "exp", -1)
    split = slots // 2 + own.shape[0] - slots
    around = [left, right, shift(left[:split], "exp", 1), shift(right[split:], "exp", -1)]
    around, out_part = lax.optimization_barrier((around, out_part))
    out_mine = lax.all_gather(out_part, "dp", axis=0)
    *sent, base = project(
        info, [own] + around, attn_gain[None], query_weight, key_weight, value_weight
    )
    mine = [sent[0]] + [shift(sent[k], "z", k) for k in range(1, RING)]
    mine = lax.optimization_barrier(mine)
    theirs = [swap(piece) for piece in mine]

    weights = (w_gate, w_up, w_down)
    theirs[-1], *weights = lax.optimization_barrier((theirs[-1], *weights))
    swapped = [swap(w) for w in weights]
    attended = attend(info, mine, theirs, slots)
    out_mine, attended = lax.optimization_barrier((out_mine, attended))
    out_theirs = swap(out_mine)
    pick, worth, segments = tabulate(info, mine, theirs, slots)
    spread = lax.all_to_all(
        attended.reshape(RING * RING, ROW, HEAD),
        ("z", "exp"),
        split_axis=0,
        concat_axis=0,
        tiled=True,
    )
    spread, pick, *swapped = lax.optimization_barrier((spread, pick, *swapped))
    kept_hidden, lent_hidden, kept, lent = mix(info, spread, out_mine, out_theirs, base, moe_gain[None])
    pieces = collect(kept) + collect(swap(lent))
    made = experts(
        info,
        segments[:, 0],
        pick,
        worth,
        kept_hidden,
        swap(lent_hidden),
        pieces,
        list(weights) + swapped,
    )
    merged = give_back(made, y, core)
    spread = jnp.stack([merged[0], swap(merged[1])]).reshape(slots, part)
    sides = jnp.stack([core, 1 - core])
    halves = (sides[:, None] + z + jnp.arange(RING, dtype=jnp.int32)[None, :]) % 2
    slots_of = jnp.where(live, own_slots, -1).reshape(RING, 2, HALF)
    slots_of = jnp.where(halves[..., None] == 0, slots_of[None, :, 0], slots_of[None, :, 1])
    slots_of = slots_of.reshape(-1)
    here = positions[:, None] == slots_of[None, :]
    placed = dot(here.astype(BF16), spread).astype(BF16)
    return jnp.where(jnp.any(here, axis=1)[:, None], placed, states)


def solution(mesh):
    dp, ctx, exp = (mesh.shape[axis] for axis in ("dp", "ctx", "exp"))
    cut = Mesh(mesh.devices.reshape(dp, ctx // 2, 2, exp), ("dp", "z", "core", "exp"))
    ctx_axes = ("z", "core")
    placed = (
        P(("dp", *ctx_axes), "exp"),
        P("dp"),
        P("dp"),
        P(),
        P(None, "exp"),
        P(None, "exp"),
        P(None, "exp"),
        P("exp", None),
        P(),
        P(("dp", *ctx_axes, "exp"), None),
        P(("dp", *ctx_axes, "exp"), None),
        P((*ctx_axes, "exp"), None, None),
        P((*ctx_axes, "exp"), None, None),
        P((*ctx_axes, "exp"), None, None),
    )
    return jax.shard_map(
        on_device,
        mesh=cut,
        in_specs=placed,
        out_specs=P(("dp", *ctx_axes), "exp"),
        check_vma=False,
    )
```

```python
import functools
import math

import jax
import jax.numpy as jnp
from jax import lax
from jax.experimental import pallas as pl
from jax.experimental.pallas import tpu as pltpu
from jax.sharding import Mesh, PartitionSpec as P

HEAD = 128
ROW = 128
HALF = 64
MOST = 48
UNIT = 256
WINDOW = 2 * MOST
SEATS = 2 * WINDOW
NOTE_LANES = 256
TILE = 256
REGION = 1920
EPS = 1e-05
RING = 4
F32 = jnp.float32
BF16 = jnp.bfloat16
AROUND = (0, -1, 1, 2)
PIECES = (4, 4, 4, 2, 2) * 2
HBM = pl.BlockSpec(memory_space=pl.ANY)
VMEM = pl.BlockSpec(memory_space=pltpu.VMEM)
SMEM = pl.BlockSpec(memory_space=pltpu.SMEM)


def dot(left, right):
    return jnp.dot(left, right, preferred_element_type=F32)


def shift(value, axis, step):
    return lax.ppermute(value, axis, [(i, (i + step) % RING) for i in range(RING)])


def ring_all(value, axis):
    return [value] + [shift(value, axis, step) for step in range(1, RING)]


def swap(value):
    return lax.ppermute(value, "core", [(0, 1), (1, 0)])


def rms(wide, gain):
    factor = lax.rsqrt(jnp.mean(wide * wide, axis=-1, keepdims=True) + EPS)
    return (wide * factor * gain).astype(BF16)


def fetch_kernel(chosen, routes, gates, states, out, held, sems):
    count, slots = sems.shape[0], chosen.shape[1]
    rows, part = held.shape[0] // count, held.shape[1]
    copies = [
        pltpu.make_async_copy(
            states.at[pl.ds(i * rows, rows), :], held.at[pl.ds(i * rows, rows), :], sems.at[i]
        )
        for i in range(count)
    ]
    for copy in copies:
        copy.start()
    parts, rest = [routes[...].astype(F32)], gates[...]
    for _ in range(3):
        parts.append(rest.astype(BF16).astype(F32))
        rest = rest - parts[-1]
    out[slots:, :] = jnp.zeros((out.shape[0] - slots, part), BF16)
    for tile in range(2):
        pair = parts[2 * tile : 2 * tile + 2]
        out[slots:, tile * ROW : (tile + 1) * ROW] = jnp.concatenate(pair, axis=0).astype(BF16)
    mine = chosen[...]
    total = None
    for i, copy in enumerate(copies):
        place = lax.broadcasted_iota(jnp.int32, (rows, slots), 0) + i * rows
        named = (place == mine).astype(F32).astype(BF16)
        copy.wait()
        some = lax.dot_general(
            named,
            held[i * rows : (i + 1) * rows, :],
            (((0,), (0,)), ((), ())),
            preferred_element_type=F32,
        )
        total = some if total is None else total + some
    out[0:slots, :] = total.astype(BF16)


def fetch(chosen, routes, gates, states):
    slots, (positions, part) = chosen.shape[1], states.shape
    return pl.pallas_call(
        fetch_kernel,
        out_shape=jax.ShapeDtypeStruct((slots + 16, part), BF16),
        in_specs=[VMEM, VMEM, VMEM, HBM],
        out_specs=VMEM,
        scratch_shapes=[pltpu.VMEM((positions, part), BF16), pltpu.SemaphoreType.DMA((4,))],
        compiler_params=pltpu.CompilerParams(vmem_limit_bytes=56 * 2**20),
        cost_estimate=pl.CostEstimate(
            flops=2 * slots * positions * part, bytes_accessed=4 * 2**20, transcendentals=0
        ),
        name="fetch",
    )(chosen, routes, gates, states)


def project_kernel(info, own, left, right, far_top, far_bottom, gain, wq, wk, wv, *rest):
    outs, base, rows, normed, weights, made, sems = (
        rest[:4],
        rest[4],
        rest[5],
        rest[6],
        rest[7],
        rest[8],
        rest[9],
    )
    z, y = info[0], info[1]
    slots = normed.shape[0]
    top, bottom = far_top.shape[0], far_bottom.shape[0]
    part = own.shape[1]

    def columns(step):
        return pl.ds(pl.multiple_of(lax.rem(y + step, RING) * part, part), part)

    copies = [
        pltpu.make_async_copy(own, rows.at[:, columns(0)], sems.at[0]),
        pltpu.make_async_copy(left, rows.at[:, columns(3)], sems.at[1]),
        pltpu.make_async_copy(right, rows.at[:, columns(1)], sems.at[2]),
        pltpu.make_async_copy(far_top, rows.at[pl.ds(0, top), columns(2)], sems.at[3]),
        pltpu.make_async_copy(far_bottom, rows.at[pl.ds(top, bottom), columns(2)], sems.at[4]),
    ]
    loads = [
        pltpu.make_async_copy(w, weights.at[i], sems.at[5 + i]) for i, w in enumerate((wq, wk, wv))
    ]
    for copy in copies + loads:
        copy.start()
    for copy in copies:
        copy.wait()

    def norm(step, _):
        at = pl.ds(pl.multiple_of(step * 64, 64), 64)
        normed[at, :] = rms(rows[at, :].astype(F32), gain[...])
        return 0

    lax.fori_loop(0, slots // 64, norm, 0)
    base[...] = rows[pl.ds(pl.multiple_of(y * ROW, ROW), ROW), :]
    for i in range(3):
        loads[i].wait()

        for step in range(slots // 256):
            at = slice(step * 256, (step + 1) * 256)
            made[at, :] = dot(normed[at, :], weights[i]).astype(BF16)
        for step, out in enumerate(outs):
            head = lax.rem(z + step, RING)
            out[0:slots, i * HEAD : (i + 1) * HEAD] = made[
                :, pl.ds(pl.multiple_of(head * HEAD, HEAD), HEAD)
            ]
    if rows.shape[0] > slots:
        lines = rows.shape[0] - slots
        for spot in range(RING * NOTE_LANES // HEAD):
            device, lane = divmod(spot * HEAD, NOTE_LANES)
            note = rows[slots:, device * part + lane : device * part + lane + HEAD]
            line, column = slots + spot // 3 * lines, spot % 3 * HEAD
            for out in outs:
                out[line : line + lines, column : column + HEAD] = note


def project(info, pieces, gain, wq, wk, wv):
    lines, part = pieces[0].shape
    slots = lines // (2 * ROW) * (2 * ROW)
    longer = slots + -(-RING * NOTE_LANES // (3 * HEAD)) * (lines - slots)
    width = gain.shape[-1]
    return pl.pallas_call(
        project_kernel,
        out_shape=[jax.ShapeDtypeStruct((longer, 3 * HEAD), BF16)] * RING
        + [jax.ShapeDtypeStruct((ROW, width), BF16)],
        in_specs=[SMEM] + [HBM] * 5 + [VMEM] + [HBM] * 3,
        out_specs=[VMEM] * 5,
        scratch_shapes=[
            pltpu.VMEM((lines, width), BF16),
            pltpu.VMEM((slots, width), BF16),
            pltpu.VMEM((3, width, part), BF16),
            pltpu.VMEM((slots, part), BF16),
            pltpu.SemaphoreType.DMA((8,)),
        ],
        compiler_params=pltpu.CompilerParams(vmem_limit_bytes=56 * 2**20),
        cost_estimate=pl.CostEstimate(
            flops=6 * slots * width * part, bytes_accessed=12 * 2**20, transcendentals=0
        ),
        name="project",
    )(info, *pieces, gain, wq, wk, wv)


def attend_kernel(info, *rest):
    mine, theirs, (out, held, sems) = rest[:RING], rest[RING : 2 * RING], rest[2 * RING :]
    z, core = info[0], info[2]
    slots = held.shape[1]
    half = slots // 2
    scale = math.log2(math.e) / HEAD**0.5
    copies = []
    for step in range(RING):
        chip = lax.rem(z + RING - step, RING)
        for source, shard in ((mine[step], 2 * chip + core), (theirs[step], 2 * chip + 1 - core)):
            source = source.at[pl.ds(0, slots), :]
            copies.append(pltpu.make_async_copy(source, held.at[shard], sems.at[len(copies)]))
    for copy in copies:
        copy.start()
    for copy in copies:
        copy.wait()

    def fold(carry, query, shard, keys, seen):
        top, mass, total = carry
        scores = (
            lax.dot_general(
                query,
                held[shard, keys, HEAD : 2 * HEAD],
                (((1,), (1,)), ((), ())),
                preferred_element_type=F32,
            )
            * scale
        )
        scores = seen(scores)
        top_new = jnp.maximum(top, jnp.max(scores, axis=1, keepdims=True))
        weights = jnp.exp2(scores - top_new)
        shrink = jnp.exp2(top - top_new)
        mass = mass * shrink + jnp.sum(weights, axis=1, keepdims=True)
        total = total * shrink + dot(weights.astype(BF16), held[shard, keys, 2 * HEAD :])
        return top_new, mass, total

    def tile(chip, own, rows):
        query = held[own, 0:rows, 0:HEAD]
        if rows < slots:
            out[chip, rows:, :] = jnp.zeros((slots - rows, HEAD), BF16)
        slot = lax.broadcasted_iota(jnp.int32, (rows, rows), 1)
        place = lax.broadcasted_iota(jnp.int32, (rows, rows), 0)
        mask = (slot <= place) & (slot < info[3 + own])
        carry = (
            jnp.full((rows, 1), -1e30, F32),
            jnp.zeros((rows, 1), F32),
            jnp.zeros((rows, HEAD), F32),
        )
        carry = fold(
            carry, query, own, slice(0, rows), lambda scores: jnp.where(mask, scores, -1e30)
        )

        def earlier(shard, state):
            slot = lax.broadcasted_iota(jnp.int32, (1, slots), 1)
            bias = jnp.where(slot < info[3 + shard], 0.0, -1e30)
            return fold(state, query, shard, slice(0, slots), lambda scores: scores + bias)

        top, mass, total = lax.fori_loop(0, own, earlier, carry)
        out[chip, 0:rows, :] = (total / mass).astype(BF16)

    def shard(chip, _):
        own = 2 * chip + core
        live = info[3 + own]

        cut = (half + slots) // 2

        @pl.when(live > cut)
        def _():
            tile(chip, own, slots)

        @pl.when((live > half) & (live <= cut))
        def _():
            tile(chip, own, cut)

        @pl.when(live <= half)
        def _():
            tile(chip, own, half)

        return 0

    lax.fori_loop(0, RING, shard, 0)


def attend(info, mine, theirs, slots):
    return pl.pallas_call(
        attend_kernel,
        out_shape=jax.ShapeDtypeStruct((RING, slots, HEAD), BF16),
        in_specs=[SMEM] + [HBM] * (len(mine) + len(theirs)),
        out_specs=VMEM,
        scratch_shapes=[
            pltpu.VMEM((2 * RING, slots, 3 * HEAD), BF16),
            pltpu.SemaphoreType.DMA((2 * RING,)),
        ],
        compiler_params=pltpu.CompilerParams(vmem_limit_bytes=56 * 2**20),
        cost_estimate=pl.CostEstimate(
            flops=20 * slots * slots * 4 * HEAD,
            bytes_accessed=4 * 2**20,
            transcendentals=20 * slots * slots,
        ),
        name="attend",
    )(info, *mine, *theirs)


def tabulate_kernel(info, *rest):
    sources, (pick, worth, segments, notes, taken, share, sems) = rest[: 2 * RING], rest[2 * RING :]
    z, y, core = info[0], info[1], info[2]
    units = pick.shape[0]
    lines = notes.shape[2]
    copies = [
        pltpu.make_async_copy(
            source.at[pl.ds(source.shape[0] - lines, lines), :],
            notes.at[i // RING, i % RING],
            sems.at[i],
        )
        for i, source in enumerate(sources)
    ]
    for copy in copies:
        copy.start()
    for copy in copies:
        copy.wait()
    lane = lax.broadcasted_iota(jnp.int32, (1, ROW), 1)
    named = [((2 * z + core) * RING + y), ((2 * z + 1 - core) * RING + y)]

    def block(index):
        side, far, near = index // 16, index // 4 % 4, index % 4
        far, near = AROUND[far] % RING, AROUND[near] % RING
        from_z = lax.rem(z + jnp.where(core == 0, far, near), RING)
        from_y = lax.rem(y + jnp.where(core == 0, near, far), RING)
        back = lax.rem(z + RING - from_z, RING)
        tiles = []
        for tile in range(2):
            spot = 2 * from_y + tile
            at = pl.ds(pl.multiple_of(spot // 3 * 16, 16), 16)
            column = pl.ds(pl.multiple_of(lax.rem(spot, 3) * HEAD, HEAD), HEAD)
            tiles.append(notes[side, back, at, column].astype(F32))
        half = lax.rem(core + from_y + from_z, 2)
        owner = 2 * from_z + (core if side == 0 else 1 - core)
        left = info[3 + owner] - from_y * ROW - half * HALF
        gates = tiles[0][8:] + (tiles[1][:8] + tiles[1][8:])
        return tiles[0][:8], gates, half, left

    for unit in range(units):
        for group in range(UNIT // ROW):
            index = 2 * (unit * (UNIT // ROW) + group)
            pair = [block(index), block(index + 1)]
            joined = []
            for part in range(2):
                first, second = (
                    jnp.where(half == at, values, pltpu.roll(values, HALF, 1))
                    for at, (values, half) in enumerate((b[part], b[2]) for b in pair)
                )
                joined.append(jnp.where(lane < HALF, first, second))
            left = jnp.where(lane < HALF, pair[0][3], pair[1][3] + HALF)
            live = jnp.where(lane < left, 1.0, 0.0)
            columns = slice(group * ROW, (group + 1) * ROW)
            for q in range(2):
                match = joined[0] == named[q].astype(F32)
                row = q * units + unit
                found = jnp.max(jnp.where(match, 1.0, 0.0), axis=0, keepdims=True)
                taken[row : row + 1, columns] = found * live
                share[row : row + 1, columns] = jnp.sum(
                    jnp.where(match, joined[1], 0.0), axis=0, keepdims=True
                )
    was = taken[...].astype(BF16)
    before = lax.broadcasted_iota(jnp.int32, (UNIT, UNIT), 0)
    after = lax.broadcasted_iota(jnp.int32, (UNIT, UNIT), 1)
    order = dot(was, (before <= after).astype(BF16))
    count = dot(was, jnp.ones((UNIT, ROW), BF16))
    filled = jnp.floor((count + 15.0) * 0.0625) * 16.0
    row = lax.broadcasted_iota(jnp.int32, (segments.shape[0], 2 * units), 0)
    other = lax.broadcasted_iota(jnp.int32, (segments.shape[0], 2 * units), 1)
    ends = row - 2 * units
    group = jnp.where(ends < 0, jnp.where(row < units, 0, 1), ends)
    same = jnp.where(other < units, 0, 1) == group
    sums = dot((same & ((ends >= 0) | (other < row))).astype(BF16), filled.astype(BF16))
    segments[...] = sums.astype(jnp.int32) + group[:, 0:1] * REGION
    taken[...] = jnp.where(taken[...] > 0.0, order - 1.0, -1.0)
    seat = lax.broadcasted_iota(jnp.int32, (WINDOW, UNIT), 0).astype(F32)
    for unit in range(units):
        for part in range(4):
            row = part % 2 * units + unit
            hit = seat + float(part // 2 * WINDOW) == taken[row : row + 1, :]
            at = slice(part * WINDOW, (part + 1) * WINDOW)
            pick[unit, at, :] = hit.astype(F32).astype(BF16)
            value = jnp.sum(jnp.where(hit, share[row : row + 1, :], 0.0), axis=1, keepdims=True)
            worth[unit, at, :] = jnp.broadcast_to(value, (WINDOW, ROW))


def tabulate(info, mine, theirs, slots):
    units = 2 * RING * RING * HALF // UNIT
    sources = list(mine) + list(theirs)
    lines = sources[0].shape[0] - slots
    return pl.pallas_call(
        tabulate_kernel,
        out_shape=[
            jax.ShapeDtypeStruct((units, 2 * SEATS, UNIT), BF16),
            jax.ShapeDtypeStruct((units, 2 * SEATS, ROW), F32),
            jax.ShapeDtypeStruct((2 * units + 8, ROW), jnp.int32),
        ],
        in_specs=[SMEM] + [HBM] * len(sources),
        out_specs=[VMEM] * 3,
        scratch_shapes=[
            pltpu.VMEM((2, RING, lines, 3 * HEAD), BF16),
            pltpu.VMEM((2 * units, UNIT), F32),
            pltpu.VMEM((2 * units, UNIT), F32),
            pltpu.SemaphoreType.DMA((2 * RING,)),
        ],
        compiler_params=pltpu.CompilerParams(vmem_limit_bytes=56 * 2**20),
        cost_estimate=pl.CostEstimate(flops=2**20, bytes_accessed=4 * 2**20, transcendentals=0),
        name="tabulate",
    )(info, *sources)


def mix_kernel(
    info, pieces, base, gain, mine, theirs, kept_hidden, lent_hidden, kept, lent, heads, total, held, sems
):
    parts, _, width = mine.shape
    core = info[2]
    copies = [
        pltpu.make_async_copy(weight.at[i], held.at[side, i], sems.at[side, i])
        for side, weight in enumerate((mine, theirs))
        for i in range(parts)
    ]
    for copy in copies:
        copy.start()
    for z in range(RING):
        for y in range(RING):
            at = (y * RING + z) * HEAD
            heads[:, at : at + HEAD] = pieces[z * RING + y]
    for i, copy in enumerate(copies):
        copy.wait()
        if i % 2 == 0:
            continue
        side, part = divmod(i, parts)
        made = [dot(heads[...], held[side, part - 1 + k]) for k in range(2)]
        for k in range(2):
            column = 2 * (part - 1 + k) + (core if side == 0 else 1 - core)
            at = pl.ds(pl.multiple_of(column * width, width), width)
            total[:, at] = base[:, at].astype(F32) + made[k]
    keep = lax.rem(info[0] + info[1] + core, 2)
    for first, hidden, normed in ((keep, kept_hidden, kept), (1 - keep, lent_hidden, lent)):
        at = pl.ds(pl.multiple_of(first * HALF, HALF), HALF)
        made = total[at, :].astype(BF16)
        hidden[...] = made
        normed[...] = rms(made.astype(F32), gain[...])


def mix(info, pieces, mine, theirs, base, gain):
    parts, depth, width = mine.shape
    whole = 2 * parts * width
    return pl.pallas_call(
        mix_kernel,
        out_shape=[jax.ShapeDtypeStruct((HALF, whole), BF16)] * 4,
        in_specs=[SMEM, VMEM, VMEM, VMEM, HBM, HBM],
        out_specs=[VMEM] * 4,
        scratch_shapes=[
            pltpu.VMEM((ROW, depth), BF16),
            pltpu.VMEM((ROW, whole), F32),
            pltpu.VMEM((2, parts, depth, width), BF16),
            pltpu.SemaphoreType.DMA((2, parts)),
        ],
        compiler_params=pltpu.CompilerParams(vmem_limit_bytes=56 * 2**20),
        cost_estimate=pl.CostEstimate(
            flops=2 * ROW * depth * whole, bytes_accessed=10 * 2**20, transcendentals=0
        ),
        name="mix",
    )(info, pieces, base, gain, mine, theirs)


def expert_kernel(info, segments, pick, worth, kept, lent, *rest):
    count = len(PIECES)
    tokens, rest = rest[:count], rest[count:]
    weights, rest = rest[:6], rest[6:]
    outs, rest = rest[:6], rest[6:]
    held, chosen, act, scale, gates, ups, downs, token_sems, weight_sems, out_sems = rest
    units = 2 * RING
    width = held.shape[-1]
    y, core = info[1], info[2]
    ff = act.shape[1]

    arriving = []
    for i, token in enumerate(tokens):
        chunk, piece = divmod(i, count // 2)
        here = held.at[chunk, piece] if piece < 3 else held.at[chunk, 3, pl.ds(2 * piece - 6, 2)]
        arriving.append(pltpu.make_async_copy(token, here, token_sems.at[i]))
        arriving[-1].start()

    def leaving(chunk, wide):
        *own, back, ahead, late_back, late_ahead = outs
        places = (
            own[chunk],
            late_back if chunk == 0 else back.at[1],
            ahead.at[1] if chunk == 0 else late_ahead,
            back.at[0] if chunk == 0 else ahead.at[0],
        )
        copies = []
        for piece, place in enumerate(places):
            for block in range(RING):
                if wide:
                    columns = pl.ds(block * (width // RING), width // RING)
                    here = held.at[chunk, piece, :, :, columns]
                else:
                    which = lax.rem(y + AROUND[piece] % RING, RING)
                    step = width // RING
                    columns = pl.ds(pl.multiple_of(which * step, step), step)
                    here = held.at[chunk, :, block, :, columns]
                sem = out_sems.at[chunk, piece, block]
                copies.append(pltpu.make_async_copy(here, place.at[block], sem))
        return copies

    loads = []
    for q in range(2):
        for i, place in enumerate((gates, ups, downs)):
            loads.append(
                pltpu.make_async_copy(
                    weights[3 * q + i].at[0], place.at[q], weight_sems.at[3 * q + i]
                )
            )

    def places(unit):
        return [pl.multiple_of(segments[q * units + unit], 16) for q in range(2)]

    def crowded(unit):
        ends = [segments[q * units + unit + 1] for q in range(2)]
        if unit == units - 1:
            ends = [segments[2 * units + q] for q in range(2)]
        used = [end - segments[q * units + unit] for q, end in enumerate(ends)]
        return jnp.maximum(used[0], used[1]) > WINDOW

    ready = 0
    for j in range(units):
        while ready < count // 2 * (j // RING) + min(j % RING, 3) + (2 if j % RING == 3 else 1):
            arriving[ready].wait()
            ready += 1
            if ready == count - 5:
                for copy in loads[:3]:
                    copy.start()
            elif ready == count:
                for copy in loads[3:]:
                    copy.start()
        starts = places(j)

        def gather(late, j=j, starts=starts):
            for q in range(2):
                at = pl.ds(starts[q] + late * WINDOW, WINDOW)
                scale[at, :] = worth[j, (2 * late + q) * WINDOW : (2 * late + q + 1) * WINDOW, :]
            for cut in range(width // 512):
                columns = slice(cut * 512, (cut + 1) * 512)
                sel = pick[j, late * SEATS : (late + 1) * SEATS, :]
                got = dot(sel, held[j // RING, j % RING, :, :, columns].reshape(UNIT, 512)).astype(BF16)
                for q in range(2):
                    at = pl.ds(starts[q] + late * WINDOW, WINDOW)
                    chosen[at, columns] = got[q * WINDOW : (q + 1) * WINDOW]

        gather(0)
        pl.when(crowded(j))(functools.partial(gather, 1))
    for q in range(2):
        end = pl.multiple_of(segments[2 * units + q], 16)
        chosen[pl.ds(end, TILE + WINDOW), :] = jnp.zeros((TILE + WINDOW, width), BF16)
        scale[pl.ds(end, TILE + WINDOW), :] = jnp.zeros((TILE + WINDOW, ROW), F32)

    for q in range(2):
        for copy in loads[3 * q : 3 * q + 3]:
            copy.wait()

        def tile(start, rows, q=q):
            at = pl.ds(pl.multiple_of(q * REGION + start, 64), rows)
            for f in range(ff // 256):
                columns = slice(f * 256, (f + 1) * 256)
                x = chosen[at, :]
                gate = dot(x, gates[q, :, columns])
                up = dot(x, ups[q, :, columns])
                act[:rows, columns] = (gate / (1.0 + jnp.exp(-gate)) * up).astype(BF16)
            for f in range(width // 512):
                columns = slice(f * 512, (f + 1) * 512)
                made = dot(act[:rows, :], downs[q, :, columns])
                chosen[at, columns] = (made * scale[at, 0:1]).astype(BF16)

        def whole(t, _):
            tile(t * TILE, TILE)
            return 0

        used = segments[2 * units + q] - q * REGION
        full = lax.div(used + TILE // 2 - 1, TILE)
        lax.fori_loop(0, full, whole, 0)

        @pl.when(used > full * TILE)
        def _():
            tile(full * TILE, TILE // 2)

    for j in range(units):
        starts = places(j)

        def combine(seats, j=j, starts=starts):
            ats = [at + late for late in range(0, seats // 2, WINDOW) for at in starts]
            for cut in range(width // 512):
                columns = slice(cut * 512, (cut + 1) * 512)
                made = jnp.concatenate([chosen[pl.ds(at, WINDOW), columns] for at in ats], axis=0)
                sums = lax.dot_general(
                    pick[j, 0:seats, :],
                    made,
                    (((0,), (0,)), ((), ())),
                    preferred_element_type=F32,
                )
                if j % RING == 0:
                    hidden = (kept if j == 0 else lent)[:, columns].astype(F32)
                    sums = jnp.concatenate([sums[:HALF] + hidden, sums[HALF:]], axis=0)
                made = sums.astype(BF16).reshape(RING, HALF, 512)
                for block in range(RING):
                    at_y = [lax.rem(y + AROUND[i] % RING, RING) for i in (j % RING, block)]
                    first = jnp.where(core == 0, j % RING, at_y[0])
                    second = jnp.where(core == 0, at_y[1], block)
                    held[j // RING, first, second, :, columns] = made[block]

        many = crowded(j)
        pl.when(many)(functools.partial(combine, 2 * SEATS))
        pl.when(jnp.logical_not(many))(functools.partial(combine, SEATS))
        if j % RING == RING - 1:
            for wide in (True, False):

                @pl.when(core == (0 if wide else 1))
                def _(j=j, wide=wide):
                    for copy in leaving(j // RING, wide):
                        copy.start()

    for wide in (True, False):

        @pl.when(core == (0 if wide else 1))
        def _(wide=wide):
            for chunk in range(2):
                for copy in leaving(chunk, wide):
                    copy.wait()


def experts(info, segments, pick, worth, kept, lent, pieces, weights):
    width = pieces[0].shape[1]
    pieces = [piece.reshape(-1, HALF, width) for piece in pieces]
    block = (RING, RING, HALF, width // RING)
    ff = weights[0].shape[2]
    return pl.pallas_call(
        expert_kernel,
        out_shape=[
            jax.ShapeDtypeStruct((*lead, *block), BF16) for lead in ((), (), (2,), (2,), (), ())
        ],
        in_specs=[SMEM, SMEM, VMEM, VMEM, VMEM, VMEM] + [HBM] * (len(pieces) + 6),
        out_specs=[HBM] * 6,
        scratch_shapes=[
            pltpu.VMEM((2, RING, RING, HALF, width), BF16),
            pltpu.VMEM((2 * REGION, width), BF16),
            pltpu.VMEM((TILE, ff), BF16),
            pltpu.VMEM((2 * REGION, ROW), F32),
            pltpu.VMEM((2, width, ff), BF16),
            pltpu.VMEM((2, width, ff), BF16),
            pltpu.VMEM((2, ff, width), BF16),
            pltpu.SemaphoreType.DMA((len(PIECES),)),
            pltpu.SemaphoreType.DMA((6,)),
            pltpu.SemaphoreType.DMA((2, RING, RING)),
        ],
        compiler_params=pltpu.CompilerParams(vmem_limit_bytes=60 * 2**20),
        cost_estimate=pl.CostEstimate(
            flops=2 * 1024 * width * ff * 3, bytes_accessed=42 * 2**20, transcendentals=2**20
        ),
        name="experts",
    )(info, segments, pick, worth, kept, lent, *pieces, *weights)


def turn(value, phase, step):
    pairs = []
    for z in range(RING):
        for core in range(2):
            for y in range(RING):
                to_z, to_y = z, y
                if (phase + core) % 2 == 0:
                    to_y = (y + step) % RING
                else:
                    to_z = (z + step) % RING
                pairs.append(((z * 2 + core) * RING + y, (to_z * 2 + core) * RING + to_y))
    return lax.ppermute(value, ("z", "core", "exp"), pairs)


def ring_gather(own, phase):
    half = own.shape[0] // 2
    before, after = turn(own, phase, 1), turn(own, phase, -1)
    return [own, before, after, turn(before[:half], phase, 1), turn(after[half:], phase, -1)]


def add(first, *others):
    total = first.astype(F32)
    for other in others:
        total = total + other.astype(F32)
    return total.astype(BF16)


def collect(own):
    near = [own, turn(own, 0, 1), turn(own, 0, -1), turn(own, 0, 2)]
    return ring_gather(jnp.concatenate(near, axis=0), 1)


def add_pair_kernel(one, to_one, two, to_two, one_out, two_out):
    one_out[...] = (one[...].astype(F32) + to_one[0].astype(F32)).astype(BF16)
    two_out[...] = (two[...].astype(F32) + to_two[0].astype(F32)).astype(BF16)


def add_pair(one, to_one, two, to_two):
    count, *rest = one.shape
    short = pl.BlockSpec((1, *rest), lambda i: (i, 0, 0, 0))
    long = pl.BlockSpec((1, 1, *rest), lambda i: (0, i, 0, 0, 0))
    return pl.pallas_call(
        add_pair_kernel,
        grid=(count,),
        out_shape=[jax.ShapeDtypeStruct(one.shape, BF16)] * 2,
        in_specs=[short, long, short, long],
        out_specs=[short, short],
        compiler_params=pltpu.CompilerParams(vmem_limit_bytes=56 * 2**20),
        cost_estimate=pl.CostEstimate(flops=2 * one.size, bytes_accessed=12 * one.size, transcendentals=0),
        name="add_pair",
    )(one, to_one, two, to_two)


def give_back(pieces, y, core):
    *own, back, ahead, late_back, late_ahead = pieces
    back, ahead = turn(back, 1, -1), turn(ahead, 1, 1)
    late_back, late_ahead = add_pair(late_back, back, late_ahead, ahead)
    late_back, late_ahead = turn(late_back, 1, -1), turn(late_ahead, 1, 1)
    sums = ((own[0], ahead[1], late_back), (own[1], back[1], late_ahead))

    def block(index):
        at = jnp.where(core == 0, (y + AROUND[index]) % RING, index)
        return jnp.stack(
            [add(*(lax.dynamic_index_in_dim(s, at, 0, keepdims=False) for s in some)) for some in sums]
        )

    return add(block(0), turn(block(1), 0, -1), turn(block(2), 0, 1), turn(block(3), 0, 2))


def on_device(
    states,
    chosen,
    counts,
    attn_gain,
    query_weight,
    key_weight,
    value_weight,
    out_weight,
    moe_gain,
    routes,
    gate_probs,
    w_gate,
    w_up,
    w_down,
):
    x, z = lax.axis_index("dp"), lax.axis_index("z")
    core, y = lax.axis_index("core"), lax.axis_index("exp")
    pos_dev, part = states.shape
    slots = chosen.shape[0] // (2 * RING)
    width = attn_gain.shape[0]
    shard = 2 * z + core
    info = jnp.concatenate([jnp.stack([z, y, core]), counts]).astype(jnp.int32)

    own_slots = lax.dynamic_slice_in_dim(chosen, shard * slots, slots)
    positions = jnp.arange(pos_dev, dtype=jnp.int32)
    own = fetch(own_slots[None], routes.T, gate_probs.T, states)
    cut = width // 8
    own, out_weight = lax.optimization_barrier((own, out_weight))
    out_part = lax.dynamic_slice_in_dim(out_weight, (2 * x + core) * cut, cut, 1)
    out_part = lax.all_gather(out_part, "exp", axis=0, tiled=True)
    left, right = shift(own, "exp", 1), shift(own, "exp", -1)
    split = slots // 2 + own.shape[0] - slots
    around = [left, right, shift(left[:split], "exp", 1), shift(right[split:], "exp", -1)]
    around, out_part = lax.optimization_barrier((around, out_part))
    out_mine = lax.all_gather(out_part, "dp", axis=0)
    *sent, base = project(
        info, [own] + around, attn_gain[None], query_weight, key_weight, value_weight
    )
    mine = [sent[0]] + [shift(sent[k], "z", k) for k in range(1, RING)]
    mine = lax.optimization_barrier(mine)
    theirs = [swap(piece) for piece in mine]

    weights = (w_gate, w_up, w_down)
    theirs[-1], *weights = lax.optimization_barrier((theirs[-1], *weights))
    swapped = [swap(w) for w in weights]
    attended = attend(info, mine, theirs, slots)
    out_mine, attended = lax.optimization_barrier((out_mine, attended))
    out_theirs = swap(out_mine)
    pick, worth, segments = tabulate(info, mine, theirs, slots)
    spread = lax.all_to_all(
        attended.reshape(RING * RING, ROW, HEAD),
        ("z", "exp"),
        split_axis=0,
        concat_axis=0,
        tiled=True,
    )
    spread, pick, chosen, counts, *swapped = lax.optimization_barrier(
        (spread, pick, chosen, counts, *swapped)
    )
    kept_hidden, lent_hidden, kept, lent = mix(info, spread, out_mine, out_theirs, base, moe_gain[None])
    pieces = collect(kept) + collect(swap(lent))
    made = experts(
        info,
        segments[:, 0],
        pick,
        worth,
        kept_hidden,
        swap(lent_hidden),
        pieces,
        list(weights) + swapped,
    )
    merged = give_back(made, y, core)
    spread = jnp.stack([merged[0], swap(merged[1])]).reshape(slots, part)
    own_slots = lax.dynamic_slice_in_dim(chosen, shard * slots, slots)
    live = jnp.arange(slots, dtype=jnp.int32) < lax.dynamic_index_in_dim(counts, shard, 0, False)
    sides = jnp.stack([core, 1 - core])
    halves = (sides[:, None] + z + jnp.arange(RING, dtype=jnp.int32)[None, :]) % 2
    slots_of = jnp.where(live, own_slots, -1).reshape(RING, 2, HALF)
    slots_of = jnp.where(halves[..., None] == 0, slots_of[None, :, 0], slots_of[None, :, 1])
    slots_of = slots_of.reshape(-1)
    here = positions[:, None] == slots_of[None, :]
    placed = dot(here.astype(BF16), spread).astype(BF16)
    return jnp.where(jnp.any(here, axis=1)[:, None], placed, states)


def solution(mesh):
    dp, ctx, exp = (mesh.shape[axis] for axis in ("dp", "ctx", "exp"))
    cut = Mesh(mesh.devices.reshape(dp, ctx // 2, 2, exp), ("dp", "z", "core", "exp"))
    ctx_axes = ("z", "core")
    placed = (
        P(("dp", *ctx_axes), "exp"),
        P("dp"),
        P("dp"),
        P(),
        P(None, "exp"),
        P(None, "exp"),
        P(None, "exp"),
        P("exp", None),
        P(),
        P(("dp", *ctx_axes, "exp"), None),
        P(("dp", *ctx_axes, "exp"), None),
        P((*ctx_axes, "exp"), None, None),
        P((*ctx_axes, "exp"), None, None),
        P((*ctx_axes, "exp"), None, None),
    )
    return jax.shard_map(
        on_device,
        mesh=cut,
        in_specs=placed,
        out_specs=P(("dp", *ctx_axes), "exp"),
        check_vma=False,
    )
```

```python
import functools
import math

import jax
import jax.numpy as jnp
from jax import lax
from jax.experimental import pallas as pl
from jax.experimental.pallas import tpu as pltpu
from jax.sharding import Mesh, PartitionSpec as P

HEAD = 128
ROW = 128
HALF = 64
MOST = 48
UNIT = 256
WINDOW = 2 * MOST
SEATS = 2 * WINDOW
NOTE_LANES = 256
TILE = 256
REGION = 1920
EPS = 1e-05
RING = 4
F32 = jnp.float32
BF16 = jnp.bfloat16
AROUND = (0, -1, 1, 2)
PIECES = (4, 4, 4, 2, 2) * 2
HBM = pl.BlockSpec(memory_space=pl.ANY)
VMEM = pl.BlockSpec(memory_space=pltpu.VMEM)
SMEM = pl.BlockSpec(memory_space=pltpu.SMEM)


def dot(left, right):
    return jnp.dot(left, right, preferred_element_type=F32)


def shift(value, axis, step):
    return lax.ppermute(value, axis, [(i, (i + step) % RING) for i in range(RING)])


def ring_all(value, axis):
    return [value] + [shift(value, axis, step) for step in range(1, RING)]


def swap(value):
    return lax.ppermute(value, "core", [(0, 1), (1, 0)])


def rms(wide, gain):
    factor = lax.rsqrt(jnp.mean(wide * wide, axis=-1, keepdims=True) + EPS)
    return (wide * factor * gain).astype(BF16)


def fetch_kernel(chosen, routes, gates, states, out, held, sems):
    count, slots = sems.shape[0], chosen.shape[1]
    rows, part = held.shape[0] // count, held.shape[1]
    copies = [
        pltpu.make_async_copy(
            states.at[pl.ds(i * rows, rows), :], held.at[pl.ds(i * rows, rows), :], sems.at[i]
        )
        for i in range(count)
    ]
    for copy in copies:
        copy.start()
    parts, rest = [routes[...].astype(F32)], gates[...]
    for _ in range(3):
        parts.append(rest.astype(BF16).astype(F32))
        rest = rest - parts[-1]
    out[slots:, :] = jnp.zeros((out.shape[0] - slots, part), BF16)
    for tile in range(2):
        pair = parts[2 * tile : 2 * tile + 2]
        out[slots:, tile * ROW : (tile + 1) * ROW] = jnp.concatenate(pair, axis=0).astype(BF16)
    mine = chosen[...]
    total = None
    for i, copy in enumerate(copies):
        place = lax.broadcasted_iota(jnp.int32, (rows, slots), 0) + i * rows
        named = (place == mine).astype(F32).astype(BF16)
        copy.wait()
        some = lax.dot_general(
            named,
            held[i * rows : (i + 1) * rows, :],
            (((0,), (0,)), ((), ())),
            preferred_element_type=F32,
        )
        total = some if total is None else total + some
    out[0:slots, :] = total.astype(BF16)


def fetch(chosen, routes, gates, states):
    slots, (positions, part) = chosen.shape[1], states.shape
    return pl.pallas_call(
        fetch_kernel,
        out_shape=jax.ShapeDtypeStruct((slots + 16, part), BF16),
        in_specs=[VMEM, VMEM, VMEM, HBM],
        out_specs=VMEM,
        scratch_shapes=[pltpu.VMEM((positions, part), BF16), pltpu.SemaphoreType.DMA((4,))],
        compiler_params=pltpu.CompilerParams(vmem_limit_bytes=56 * 2**20),
        cost_estimate=pl.CostEstimate(
            flops=2 * slots * positions * part, bytes_accessed=4 * 2**20, transcendentals=0
        ),
        name="fetch",
    )(chosen, routes, gates, states)


def project_kernel(info, own, left, right, far_top, far_bottom, gain, wq, wk, wv, *rest):
    outs, base, rows, normed, weights, made, sems = (
        rest[:4],
        rest[4],
        rest[5],
        rest[6],
        rest[7],
        rest[8],
        rest[9],
    )
    z, y = info[0], info[1]
    slots = normed.shape[0]
    top, bottom = far_top.shape[0], far_bottom.shape[0]
    part = own.shape[1]

    def columns(step):
        return pl.ds(pl.multiple_of(lax.rem(y + step, RING) * part, part), part)

    copies = [
        pltpu.make_async_copy(own, rows.at[:, columns(0)], sems.at[0]),
        pltpu.make_async_copy(left, rows.at[:, columns(3)], sems.at[1]),
        pltpu.make_async_copy(right, rows.at[:, columns(1)], sems.at[2]),
        pltpu.make_async_copy(far_top, rows.at[pl.ds(0, top), columns(2)], sems.at[3]),
        pltpu.make_async_copy(far_bottom, rows.at[pl.ds(top, bottom), columns(2)], sems.at[4]),
    ]
    loads = [
        pltpu.make_async_copy(w, weights.at[i], sems.at[5 + i]) for i, w in enumerate((wq, wk, wv))
    ]
    for copy in copies + loads:
        copy.start()
    for copy in copies:
        copy.wait()

    def norm(step, _):
        at = pl.ds(pl.multiple_of(step * 64, 64), 64)
        normed[at, :] = rms(rows[at, :].astype(F32), gain[...])
        return 0

    lax.fori_loop(0, slots // 64, norm, 0)
    base[...] = rows[pl.ds(pl.multiple_of(y * ROW, ROW), ROW), :]
    for i in range(3):
        loads[i].wait()

        for step in range(slots // 256):
            at = slice(step * 256, (step + 1) * 256)
            made[at, :] = dot(normed[at, :], weights[i]).astype(BF16)
        for step, out in enumerate(outs):
            head = lax.rem(z + step, RING)
            out[0:slots, i * HEAD : (i + 1) * HEAD] = made[
                :, pl.ds(pl.multiple_of(head * HEAD, HEAD), HEAD)
            ]
    if rows.shape[0] > slots:
        lines = rows.shape[0] - slots
        for spot in range(RING * NOTE_LANES // HEAD):
            device, lane = divmod(spot * HEAD, NOTE_LANES)
            note = rows[slots:, device * part + lane : device * part + lane + HEAD]
            line, column = slots + spot // 3 * lines, spot % 3 * HEAD
            for out in outs:
                out[line : line + lines, column : column + HEAD] = note


def project(info, pieces, gain, wq, wk, wv):
    lines, part = pieces[0].shape
    slots = lines // (2 * ROW) * (2 * ROW)
    longer = slots + -(-RING * NOTE_LANES // (3 * HEAD)) * (lines - slots)
    width = gain.shape[-1]
    return pl.pallas_call(
        project_kernel,
        out_shape=[jax.ShapeDtypeStruct((longer, 3 * HEAD), BF16)] * RING
        + [jax.ShapeDtypeStruct((ROW, width), BF16)],
        in_specs=[SMEM] + [HBM] * 5 + [VMEM] + [HBM] * 3,
        out_specs=[VMEM] * 5,
        scratch_shapes=[
            pltpu.VMEM((lines, width), BF16),
            pltpu.VMEM((slots, width), BF16),
            pltpu.VMEM((3, width, part), BF16),
            pltpu.VMEM((slots, part), BF16),
            pltpu.SemaphoreType.DMA((8,)),
        ],
        compiler_params=pltpu.CompilerParams(vmem_limit_bytes=56 * 2**20),
        cost_estimate=pl.CostEstimate(
            flops=6 * slots * width * part, bytes_accessed=12 * 2**20, transcendentals=0
        ),
        name="project",
    )(info, *pieces, gain, wq, wk, wv)


def attend_kernel(info, *rest):
    mine, theirs, (out, held, sems) = rest[:RING], rest[RING : 2 * RING], rest[2 * RING :]
    z, core = info[0], info[2]
    slots = held.shape[1]
    half = slots // 2
    scale = math.log2(math.e) / HEAD**0.5
    copies = []
    for step in range(RING):
        chip = lax.rem(z + RING - step, RING)
        for source, shard in ((mine[step], 2 * chip + core), (theirs[step], 2 * chip + 1 - core)):
            source = source.at[pl.ds(0, slots), :]
            copies.append(pltpu.make_async_copy(source, held.at[shard], sems.at[len(copies)]))
    for copy in copies:
        copy.start()
    for copy in copies:
        copy.wait()

    def fold(carry, query, shard, keys, seen):
        top, mass, total = carry
        scores = (
            lax.dot_general(
                query,
                held[shard, keys, HEAD : 2 * HEAD],
                (((1,), (1,)), ((), ())),
                preferred_element_type=F32,
            )
            * scale
        )
        scores = seen(scores)
        top_new = jnp.maximum(top, jnp.max(scores, axis=1, keepdims=True))
        weights = jnp.exp2(scores - top_new)
        shrink = jnp.exp2(top - top_new)
        mass = mass * shrink + jnp.sum(weights, axis=1, keepdims=True)
        total = total * shrink + dot(weights.astype(BF16), held[shard, keys, 2 * HEAD :])
        return top_new, mass, total

    def tile(chip, own, rows):
        query = held[own, 0:rows, 0:HEAD]
        if rows < slots:
            out[chip, rows:, :] = jnp.zeros((slots - rows, HEAD), BF16)
        slot = lax.broadcasted_iota(jnp.int32, (rows, rows), 1)
        place = lax.broadcasted_iota(jnp.int32, (rows, rows), 0)
        mask = (slot <= place) & (slot < info[3 + own])
        carry = (
            jnp.full((rows, 1), -1e30, F32),
            jnp.zeros((rows, 1), F32),
            jnp.zeros((rows, HEAD), F32),
        )
        carry = fold(
            carry, query, own, slice(0, rows), lambda scores: jnp.where(mask, scores, -1e30)
        )

        def earlier(shard, state):
            slot = lax.broadcasted_iota(jnp.int32, (1, slots), 1)
            bias = jnp.where(slot < info[3 + shard], 0.0, -1e30)
            return fold(state, query, shard, slice(0, slots), lambda scores: scores + bias)

        top, mass, total = lax.fori_loop(0, own, earlier, carry)
        out[chip, 0:rows, :] = (total / mass).astype(BF16)

    def shard(chip, _):
        own = 2 * chip + core
        live = info[3 + own]

        cut = (half + slots) // 2

        @pl.when(live > cut)
        def _():
            tile(chip, own, slots)

        @pl.when((live > half) & (live <= cut))
        def _():
            tile(chip, own, cut)

        @pl.when(live <= half)
        def _():
            tile(chip, own, half)

        return 0

    lax.fori_loop(0, RING, shard, 0)


def attend(info, mine, theirs, slots):
    return pl.pallas_call(
        attend_kernel,
        out_shape=jax.ShapeDtypeStruct((RING, slots, HEAD), BF16),
        in_specs=[SMEM] + [HBM] * (len(mine) + len(theirs)),
        out_specs=VMEM,
        scratch_shapes=[
            pltpu.VMEM((2 * RING, slots, 3 * HEAD), BF16),
            pltpu.SemaphoreType.DMA((2 * RING,)),
        ],
        compiler_params=pltpu.CompilerParams(vmem_limit_bytes=56 * 2**20),
        cost_estimate=pl.CostEstimate(
            flops=20 * slots * slots * 4 * HEAD,
            bytes_accessed=4 * 2**20,
            transcendentals=20 * slots * slots,
        ),
        name="attend",
    )(info, *mine, *theirs)


def tabulate_kernel(info, *rest):
    sources, (pick, worth, segments, notes, taken, share, sems) = rest[: 2 * RING], rest[2 * RING :]
    z, y, core = info[0], info[1], info[2]
    units = pick.shape[0]
    lines = notes.shape[2]
    copies = [
        pltpu.make_async_copy(
            source.at[pl.ds(source.shape[0] - lines, lines), :],
            notes.at[i // RING, i % RING],
            sems.at[i],
        )
        for i, source in enumerate(sources)
    ]
    for copy in copies:
        copy.start()
    for copy in copies:
        copy.wait()
    lane = lax.broadcasted_iota(jnp.int32, (1, ROW), 1)
    named = [((2 * z + core) * RING + y), ((2 * z + 1 - core) * RING + y)]

    def block(index):
        side, far, near = index // 16, index // 4 % 4, index % 4
        far, near = AROUND[far] % RING, AROUND[near] % RING
        from_z = lax.rem(z + jnp.where(core == 0, far, near), RING)
        from_y = lax.rem(y + jnp.where(core == 0, near, far), RING)
        back = lax.rem(z + RING - from_z, RING)
        tiles = []
        for tile in range(2):
            spot = 2 * from_y + tile
            at = pl.ds(pl.multiple_of(spot // 3 * 16, 16), 16)
            column = pl.ds(pl.multiple_of(lax.rem(spot, 3) * HEAD, HEAD), HEAD)
            tiles.append(notes[side, back, at, column].astype(F32))
        half = lax.rem(core + from_y + from_z, 2)
        owner = 2 * from_z + (core if side == 0 else 1 - core)
        left = info[3 + owner] - from_y * ROW - half * HALF
        gates = tiles[0][8:] + (tiles[1][:8] + tiles[1][8:])
        return tiles[0][:8], gates, half, left

    for unit in range(units):
        for group in range(UNIT // ROW):
            index = 2 * (unit * (UNIT // ROW) + group)
            pair = [block(index), block(index + 1)]
            joined = []
            for part in range(2):
                first, second = (
                    jnp.where(half == at, values, pltpu.roll(values, HALF, 1))
                    for at, (values, half) in enumerate((b[part], b[2]) for b in pair)
                )
                joined.append(jnp.where(lane < HALF, first, second))
            left = jnp.where(lane < HALF, pair[0][3], pair[1][3] + HALF)
            live = jnp.where(lane < left, 1.0, 0.0)
            columns = slice(group * ROW, (group + 1) * ROW)
            for q in range(2):
                match = joined[0] == named[q].astype(F32)
                row = q * units + unit
                found = jnp.max(jnp.where(match, 1.0, 0.0), axis=0, keepdims=True)
                taken[row : row + 1, columns] = found * live
                share[row : row + 1, columns] = jnp.sum(
                    jnp.where(match, joined[1], 0.0), axis=0, keepdims=True
                )
    was = taken[...].astype(BF16)
    before = lax.broadcasted_iota(jnp.int32, (UNIT, UNIT), 0)
    after = lax.broadcasted_iota(jnp.int32, (UNIT, UNIT), 1)
    order = dot(was, (before <= after).astype(BF16))
    count = dot(was, jnp.ones((UNIT, ROW), BF16))
    filled = jnp.floor((count + 15.0) * 0.0625) * 16.0
    row = lax.broadcasted_iota(jnp.int32, (segments.shape[0], 2 * units), 0)
    other = lax.broadcasted_iota(jnp.int32, (segments.shape[0], 2 * units), 1)
    ends = row - 2 * units
    group = jnp.where(ends < 0, jnp.where(row < units, 0, 1), ends)
    same = jnp.where(other < units, 0, 1) == group
    sums = dot((same & ((ends >= 0) | (other < row))).astype(BF16), filled.astype(BF16))
    segments[...] = sums.astype(jnp.int32) + group[:, 0:1] * REGION
    taken[...] = jnp.where(taken[...] > 0.0, order - 1.0, -1.0)
    seat = lax.broadcasted_iota(jnp.int32, (WINDOW, UNIT), 0).astype(F32)
    for unit in range(units):
        for part in range(4):
            row = part % 2 * units + unit
            hit = seat + float(part // 2 * WINDOW) == taken[row : row + 1, :]
            at = slice(part * WINDOW, (part + 1) * WINDOW)
            pick[unit, at, :] = hit.astype(F32).astype(BF16)
            value = jnp.sum(jnp.where(hit, share[row : row + 1, :], 0.0), axis=1, keepdims=True)
            worth[unit, at, :] = jnp.broadcast_to(value, (WINDOW, ROW))


def tabulate(info, mine, theirs, slots):
    units = 2 * RING * RING * HALF // UNIT
    sources = list(mine) + list(theirs)
    lines = sources[0].shape[0] - slots
    return pl.pallas_call(
        tabulate_kernel,
        out_shape=[
            jax.ShapeDtypeStruct((units, 2 * SEATS, UNIT), BF16),
            jax.ShapeDtypeStruct((units, 2 * SEATS, ROW), F32),
            jax.ShapeDtypeStruct((2 * units + 8, ROW), jnp.int32),
        ],
        in_specs=[SMEM] + [HBM] * len(sources),
        out_specs=[VMEM] * 3,
        scratch_shapes=[
            pltpu.VMEM((2, RING, lines, 3 * HEAD), BF16),
            pltpu.VMEM((2 * units, UNIT), F32),
            pltpu.VMEM((2 * units, UNIT), F32),
            pltpu.SemaphoreType.DMA((2 * RING,)),
        ],
        compiler_params=pltpu.CompilerParams(vmem_limit_bytes=56 * 2**20),
        cost_estimate=pl.CostEstimate(flops=2**20, bytes_accessed=4 * 2**20, transcendentals=0),
        name="tabulate",
    )(info, *sources)


def mix_kernel(
    info, pieces, base, gain, mine, theirs, kept_hidden, lent_hidden, kept, lent, heads, total, held, sems
):
    parts, _, width = mine.shape
    core = info[2]
    copies = [
        pltpu.make_async_copy(weight.at[i], held.at[side, i], sems.at[side, i])
        for side, weight in enumerate((mine, theirs))
        for i in range(parts)
    ]
    for copy in copies:
        copy.start()
    for z in range(RING):
        for y in range(RING):
            at = (y * RING + z) * HEAD
            heads[:, at : at + HEAD] = pieces[z * RING + y]
    for i, copy in enumerate(copies):
        copy.wait()
        if i % 2 == 0:
            continue
        side, part = divmod(i, parts)
        made = [dot(heads[...], held[side, part - 1 + k]) for k in range(2)]
        for k in range(2):
            column = 2 * (part - 1 + k) + (core if side == 0 else 1 - core)
            at = pl.ds(pl.multiple_of(column * width, width), width)
            total[:, at] = base[:, at].astype(F32) + made[k]
    keep = lax.rem(info[0] + info[1] + core, 2)
    for first, hidden, normed in ((keep, kept_hidden, kept), (1 - keep, lent_hidden, lent)):
        at = pl.ds(pl.multiple_of(first * HALF, HALF), HALF)
        made = total[at, :].astype(BF16)
        hidden[...] = made
        normed[...] = rms(made.astype(F32), gain[...])


def mix(info, pieces, mine, theirs, base, gain):
    parts, depth, width = mine.shape
    whole = 2 * parts * width
    return pl.pallas_call(
        mix_kernel,
        out_shape=[jax.ShapeDtypeStruct((HALF, whole), BF16)] * 4,
        in_specs=[SMEM, VMEM, VMEM, VMEM, HBM, HBM],
        out_specs=[VMEM] * 4,
        scratch_shapes=[
            pltpu.VMEM((ROW, depth), BF16),
            pltpu.VMEM((ROW, whole), F32),
            pltpu.VMEM((2, parts, depth, width), BF16),
            pltpu.SemaphoreType.DMA((2, parts)),
        ],
        compiler_params=pltpu.CompilerParams(vmem_limit_bytes=56 * 2**20),
        cost_estimate=pl.CostEstimate(
            flops=2 * ROW * depth * whole, bytes_accessed=10 * 2**20, transcendentals=0
        ),
        name="mix",
    )(info, pieces, base, gain, mine, theirs)


def expert_kernel(info, segments, pick, worth, kept, lent, *rest):
    count = len(PIECES)
    tokens, rest = rest[:count], rest[count:]
    weights, rest = rest[:6], rest[6:]
    outs, rest = rest[:6], rest[6:]
    held, chosen, act, scale, gates, ups, downs, token_sems, weight_sems, out_sems = rest
    units = 2 * RING
    width = held.shape[-1]
    y, core = info[1], info[2]
    ff = act.shape[1]

    arriving = []
    for i, token in enumerate(tokens):
        chunk, piece = divmod(i, count // 2)
        here = held.at[chunk, piece] if piece < 3 else held.at[chunk, 3, pl.ds(2 * piece - 6, 2)]
        arriving.append(pltpu.make_async_copy(token, here, token_sems.at[i]))
        arriving[-1].start()

    def leaving(chunk, wide):
        *own, back, ahead, late_back, late_ahead = outs
        places = (
            own[chunk],
            late_back if chunk == 0 else back.at[1],
            ahead.at[1] if chunk == 0 else late_ahead,
            back.at[0] if chunk == 0 else ahead.at[0],
        )
        copies = []
        for piece, place in enumerate(places):
            for block in range(RING):
                if wide:
                    columns = pl.ds(block * (width // RING), width // RING)
                    here = held.at[chunk, piece, :, :, columns]
                else:
                    which = lax.rem(y + AROUND[piece] % RING, RING)
                    step = width // RING
                    columns = pl.ds(pl.multiple_of(which * step, step), step)
                    here = held.at[chunk, :, block, :, columns]
                sem = out_sems.at[chunk, piece, block]
                copies.append(pltpu.make_async_copy(here, place.at[block], sem))
        return copies

    loads = []
    for q in range(2):
        for i, place in enumerate((gates, ups, downs)):
            loads.append(
                pltpu.make_async_copy(
                    weights[3 * q + i].at[0], place.at[q], weight_sems.at[3 * q + i]
                )
            )

    def places(unit):
        return [pl.multiple_of(segments[q * units + unit], 16) for q in range(2)]

    def crowded(unit):
        ends = [segments[q * units + unit + 1] for q in range(2)]
        if unit == units - 1:
            ends = [segments[2 * units + q] for q in range(2)]
        used = [end - segments[q * units + unit] for q, end in enumerate(ends)]
        return jnp.maximum(used[0], used[1]) > WINDOW

    ready = 0
    for j in range(units):
        while ready < count // 2 * (j // RING) + min(j % RING, 3) + (2 if j % RING == 3 else 1):
            arriving[ready].wait()
            ready += 1
            if ready == count - 5:
                for copy in loads[:3]:
                    copy.start()
            elif ready == count:
                for copy in loads[3:]:
                    copy.start()
        starts = places(j)

        def gather(late, j=j, starts=starts):
            for q in range(2):
                at = pl.ds(starts[q] + late * WINDOW, WINDOW)
                scale[at, :] = worth[j, (2 * late + q) * WINDOW : (2 * late + q + 1) * WINDOW, :]
            for cut in range(width // 512):
                columns = slice(cut * 512, (cut + 1) * 512)
                sel = pick[j, late * SEATS : (late + 1) * SEATS, :]
                got = dot(sel, held[j // RING, j % RING, :, :, columns].reshape(UNIT, 512)).astype(BF16)
                for q in range(2):
                    at = pl.ds(starts[q] + late * WINDOW, WINDOW)
                    chosen[at, columns] = got[q * WINDOW : (q + 1) * WINDOW]

        gather(0)
        pl.when(crowded(j))(functools.partial(gather, 1))
    for q in range(2):
        end = pl.multiple_of(segments[2 * units + q], 16)
        chosen[pl.ds(end, TILE + WINDOW), :] = jnp.zeros((TILE + WINDOW, width), BF16)
        scale[pl.ds(end, TILE + WINDOW), :] = jnp.zeros((TILE + WINDOW, ROW), F32)

    for q in range(2):
        for copy in loads[3 * q : 3 * q + 3]:
            copy.wait()

        def tile(start, rows, q=q):
            at = pl.ds(pl.multiple_of(q * REGION + start, 64), rows)
            for f in range(ff // 256):
                columns = slice(f * 256, (f + 1) * 256)
                x = chosen[at, :]
                gate = dot(x, gates[q, :, columns])
                up = dot(x, ups[q, :, columns])
                act[:rows, columns] = (gate / (1.0 + jnp.exp(-gate)) * up).astype(BF16)
            for f in range(width // 512):
                columns = slice(f * 512, (f + 1) * 512)
                made = dot(act[:rows, :], downs[q, :, columns])
                chosen[at, columns] = (made * scale[at, 0:1]).astype(BF16)

        def whole(t, _):
            tile(t * TILE, TILE)
            return 0

        used = segments[2 * units + q] - q * REGION
        full = lax.div(used + TILE // 2 - 1, TILE)
        lax.fori_loop(0, full, whole, 0)

        @pl.when(used > full * TILE)
        def _():
            tile(full * TILE, TILE // 2)

    for j in range(units):
        starts = places(j)

        def combine(seats, j=j, starts=starts):
            ats = [at + late for late in range(0, seats // 2, WINDOW) for at in starts]
            for cut in range(width // 512):
                columns = slice(cut * 512, (cut + 1) * 512)
                made = jnp.concatenate([chosen[pl.ds(at, WINDOW), columns] for at in ats], axis=0)
                sums = lax.dot_general(
                    pick[j, 0:seats, :],
                    made,
                    (((0,), (0,)), ((), ())),
                    preferred_element_type=F32,
                )
                if j % RING == 0:
                    hidden = (kept if j == 0 else lent)[:, columns].astype(F32)
                    sums = jnp.concatenate([sums[:HALF] + hidden, sums[HALF:]], axis=0)
                made = sums.astype(BF16).reshape(RING, HALF, 512)
                for block in range(RING):
                    at_y = [lax.rem(y + AROUND[i] % RING, RING) for i in (j % RING, block)]
                    first = jnp.where(core == 0, j % RING, at_y[0])
                    second = jnp.where(core == 0, at_y[1], block)
                    held[j // RING, first, second, :, columns] = made[block]

        many = crowded(j)
        pl.when(many)(functools.partial(combine, 2 * SEATS))
        pl.when(jnp.logical_not(many))(functools.partial(combine, SEATS))
        if j % RING == RING - 1:
            for wide in (True, False):

                @pl.when(core == (0 if wide else 1))
                def _(j=j, wide=wide):
                    for copy in leaving(j // RING, wide):
                        copy.start()

    for wide in (True, False):

        @pl.when(core == (0 if wide else 1))
        def _(wide=wide):
            for chunk in range(2):
                for copy in leaving(chunk, wide):
                    copy.wait()


def experts(info, segments, pick, worth, kept, lent, pieces, weights):
    width = pieces[0].shape[1]
    pieces = [piece.reshape(-1, HALF, width) for piece in pieces]
    block = (RING, RING, HALF, width // RING)
    ff = weights[0].shape[2]
    return pl.pallas_call(
        expert_kernel,
        out_shape=[
            jax.ShapeDtypeStruct((*lead, *block), BF16) for lead in ((), (), (2,), (2,), (), ())
        ],
        in_specs=[SMEM, SMEM, VMEM, VMEM, VMEM, VMEM] + [HBM] * (len(pieces) + 6),
        out_specs=[HBM] * 6,
        scratch_shapes=[
            pltpu.VMEM((2, RING, RING, HALF, width), BF16),
            pltpu.VMEM((2 * REGION, width), BF16),
            pltpu.VMEM((TILE, ff), BF16),
            pltpu.VMEM((2 * REGION, ROW), F32),
            pltpu.VMEM((2, width, ff), BF16),
            pltpu.VMEM((2, width, ff), BF16),
            pltpu.VMEM((2, ff, width), BF16),
            pltpu.SemaphoreType.DMA((len(PIECES),)),
            pltpu.SemaphoreType.DMA((6,)),
            pltpu.SemaphoreType.DMA((2, RING, RING)),
        ],
        compiler_params=pltpu.CompilerParams(vmem_limit_bytes=60 * 2**20),
        cost_estimate=pl.CostEstimate(
            flops=2 * 1024 * width * ff * 3, bytes_accessed=42 * 2**20, transcendentals=2**20
        ),
        name="experts",
    )(info, segments, pick, worth, kept, lent, *pieces, *weights)


def turn(value, phase, step):
    pairs = []
    for z in range(RING):
        for core in range(2):
            for y in range(RING):
                to_z, to_y = z, y
                if (phase + core) % 2 == 0:
                    to_y = (y + step) % RING
                else:
                    to_z = (z + step) % RING
                pairs.append(((z * 2 + core) * RING + y, (to_z * 2 + core) * RING + to_y))
    return lax.ppermute(value, ("z", "core", "exp"), pairs)


def ring_gather(own, phase):
    half = own.shape[0] // 2
    before, after = turn(own, phase, 1), turn(own, phase, -1)
    return [own, before, after, turn(before[:half], phase, 1), turn(after[half:], phase, -1)]


def add(first, *others):
    total = first.astype(F32)
    for other in others:
        total = total + other.astype(F32)
    return total.astype(BF16)


def collect(own):
    near = [own, turn(own, 0, 1), turn(own, 0, -1), turn(own, 0, 2)]
    return ring_gather(jnp.concatenate(near, axis=0), 1)


def give_back(pieces, y, core):
    *own, back, ahead, late_back, late_ahead = pieces
    back, ahead = turn(back, 1, -1), turn(ahead, 1, 1)
    late_back = turn(add(late_back, back[0]), 1, -1)
    late_ahead = turn(add(late_ahead, ahead[0]), 1, 1)
    sums = ((own[0], ahead[1], late_back), (own[1], back[1], late_ahead))

    def block(index):
        at = jnp.where(core == 0, (y + AROUND[index]) % RING, index)
        return jnp.stack(
            [add(*(lax.dynamic_index_in_dim(s, at, 0, keepdims=False) for s in some)) for some in sums]
        )

    return add(block(0), turn(block(1), 0, -1), turn(block(2), 0, 1), turn(block(3), 0, 2))


def on_device(
    states,
    chosen,
    counts,
    attn_gain,
    query_weight,
    key_weight,
    value_weight,
    out_weight,
    moe_gain,
    routes,
    gate_probs,
    w_gate,
    w_up,
    w_down,
):
    x, z = lax.axis_index("dp"), lax.axis_index("z")
    core, y = lax.axis_index("core"), lax.axis_index("exp")
    pos_dev, part = states.shape
    slots = chosen.shape[0] // (2 * RING)
    width = attn_gain.shape[0]
    shard = 2 * z + core
    info = jnp.concatenate([jnp.stack([z, y, core]), counts]).astype(jnp.int32)

    own_slots = lax.dynamic_slice_in_dim(chosen, shard * slots, slots)
    positions = jnp.arange(pos_dev, dtype=jnp.int32)
    own = fetch(own_slots[None], routes.T, gate_probs.T, states)
    cut = width // 8
    own, out_weight = lax.optimization_barrier((own, out_weight))
    out_part = lax.dynamic_slice_in_dim(out_weight, (2 * x + core) * cut, cut, 1)
    out_part = lax.all_gather(out_part, "exp", axis=0, tiled=True)
    left, right = shift(own, "exp", 1), shift(own, "exp", -1)
    split = slots // 2 + own.shape[0] - slots
    around = [left, right, shift(left[:split], "exp", 1), shift(right[split:], "exp", -1)]
    around, out_part = lax.optimization_barrier((around, out_part))
    out_mine = lax.all_gather(out_part, "dp", axis=0)
    *sent, base = project(
        info, [own] + around, attn_gain[None], query_weight, key_weight, value_weight
    )
    mine = [sent[0]] + [shift(sent[k], "z", k) for k in range(1, RING)]
    mine = lax.optimization_barrier(mine)
    theirs = [swap(piece) for piece in mine]

    weights = (w_gate, w_up, w_down)
    theirs[-1], *weights = lax.optimization_barrier((theirs[-1], *weights))
    swapped = [swap(w) for w in weights]
    attended = attend(info, mine, theirs, slots)
    info, attended = lax.optimization_barrier((info, attended))
    pick, worth, segments = tabulate(info, mine, theirs, slots)
    out_mine, pick = lax.optimization_barrier((out_mine, pick))
    out_theirs = swap(out_mine)
    spread = lax.all_to_all(
        attended.reshape(RING * RING, ROW, HEAD),
        ("z", "exp"),
        split_axis=0,
        concat_axis=0,
        tiled=True,
    )
    spread, pick, chosen, counts, *swapped = lax.optimization_barrier(
        (spread, pick, chosen, counts, *swapped)
    )
    kept_hidden, lent_hidden, kept, lent = mix(info, spread, out_mine, out_theirs, base, moe_gain[None])
    pieces = collect(kept) + collect(swap(lent))
    made = experts(
        info,
        segments[:, 0],
        pick,
        worth,
        kept_hidden,
        swap(lent_hidden),
        pieces,
        list(weights) + swapped,
    )
    merged = give_back(made, y, core)
    spread = jnp.stack([merged[0], swap(merged[1])]).reshape(slots, part)
    own_slots = lax.dynamic_slice_in_dim(chosen, shard * slots, slots)
    live = jnp.arange(slots, dtype=jnp.int32) < lax.dynamic_index_in_dim(counts, shard, 0, False)
    sides = jnp.stack([core, 1 - core])
    halves = (sides[:, None] + z + jnp.arange(RING, dtype=jnp.int32)[None, :]) % 2
    slots_of = jnp.where(live, own_slots, -1).reshape(RING, 2, HALF)
    slots_of = jnp.where(halves[..., None] == 0, slots_of[None, :, 0], slots_of[None, :, 1])
    slots_of = slots_of.reshape(-1)
    here = positions[:, None] == slots_of[None, :]
    placed = dot(here.astype(BF16), spread).astype(BF16)
    return jnp.where(jnp.any(here, axis=1)[:, None], placed, states)


def solution(mesh):
    dp, ctx, exp = (mesh.shape[axis] for axis in ("dp", "ctx", "exp"))
    cut = Mesh(mesh.devices.reshape(dp, ctx // 2, 2, exp), ("dp", "z", "core", "exp"))
    ctx_axes = ("z", "core")
    placed = (
        P(("dp", *ctx_axes), "exp"),
        P("dp"),
        P("dp"),
        P(),
        P(None, "exp"),
        P(None, "exp"),
        P(None, "exp"),
        P("exp", None),
        P(),
        P(("dp", *ctx_axes, "exp"), None),
        P(("dp", *ctx_axes, "exp"), None),
        P((*ctx_axes, "exp"), None, None),
        P((*ctx_axes, "exp"), None, None),
        P((*ctx_axes, "exp"), None, None),
    )
    return jax.shard_map(
        on_device,
        mesh=cut,
        in_specs=placed,
        out_specs=P(("dp", *ctx_axes), "exp"),
        check_vma=False,
    )
```
